32 devices in a mesh: dp: 8 (over y, x, core), ctx: 4 (over z).
Axes of the slice: x: 2, y: 2, z: 4, core: 2. Of those that a mesh axis runs over, the one named last changes fastest.
Arguments:
- tokens: bfloat16 [16384, 1024], P(('dp', 'ctx')), may hold values from -6 to 6
- lengths: int32 [8], P('dp'), may hold values from 512 to 2048, as said below
- cotangent: bfloat16 [16384, 1024], P(('dp', 'ctx')), may hold values from -6 to 6
- query_proj: float32 [1024, 1024], P(('dp', 'ctx')), may hold values from -0.375 to 0.375
- query_offset: float32 [1024], P(('dp', 'ctx')), may hold values from -2 to 2
- key_proj: float32 [1024, 1024], P(('dp', 'ctx')), may hold values from -0.1875 to 0.1875
- value_proj: float32 [1024, 1024], P(('dp', 'ctx')), may hold values from -0.1875 to 0.1875
- value_offset: float32 [1024], P(('dp', 'ctx')), may hold values from -0.3 to 0.3
- attn_proj: float32 [1024, 1024], P(('dp', 'ctx')), may hold values from -1.5 to 1.5
- attn_offset: float32 [1024], P(('dp', 'ctx')), may hold values from -2 to 2
- attn_gain: float32 [1024], P(('dp', 'ctx')), may hold values from 0.1 to 1.9
- attn_shift: float32 [1024], P(('dp', 'ctx')), may hold values from -2 to 2
- inner_proj: float32 [1024, 4096], P(('dp', 'ctx')), may hold values from -0.1875 to 0.1875
- inner_offset: float32 [4096], P(('dp', 'ctx')), may hold values from -2 to 2
- outer_proj: float32 [4096, 1024], P(('dp', 'ctx')), may hold values from -0.09375 to 0.09375
- outer_offset: float32 [1024], P(('dp', 'ctx')), may hold values from -2 to 2
- final_gain: float32 [1024], P(('dp', 'ctx')), may hold values from 0.1 to 1.9
- final_shift: float32 [1024], P(('dp', 'ctx')), may hold values from -2 to 2
Outputs:
- layer_out: bfloat16 [16384, 1024], P(('dp', 'ctx'))
- input_grad: bfloat16 [16384, 1024], P(('dp', 'ctx'))
- grad_query_proj: float32 [1024, 1024], P(('dp', 'ctx'))
- grad_query_offset: float32 [1024], P(('dp', 'ctx'))
- grad_key_proj: float32 [1024, 1024], P(('dp', 'ctx'))
- grad_value_proj: float32 [1024, 1024], P(('dp', 'ctx'))
- grad_value_offset: float32 [1024], P(('dp', 'ctx'))
- grad_attn_proj: float32 [1024, 1024], P(('dp', 'ctx'))
- grad_attn_offset: float32 [1024], P(('dp', 'ctx'))
- grad_attn_gain: float32 [1024], P(('dp', 'ctx'))
- grad_attn_shift: float32 [1024], P(('dp', 'ctx'))
- grad_inner_proj: float32 [1024, 4096], P(('dp', 'ctx'))
- grad_inner_offset: float32 [4096], P(('dp', 'ctx'))
- grad_outer_proj: float32 [4096, 1024], P(('dp', 'ctx'))
- grad_outer_offset: float32 [1024], P(('dp', 'ctx'))
- grad_final_gain: float32 [1024], P(('dp', 'ctx'))
- grad_final_shift: float32 [1024], P(('dp', 'ctx'))
The draws below stay inside these ranges and needn't reach their ends.
Inputs may be any that keep to these rules, and one draw needn't show every extreme that they name: Sequence b holds lengths[b] real tokens followed by padding; some sequence has all 2048 tokens and some other has exactly 512.
All inputs are finite; a program needn't handle non-finite values.
Results may differ from the reference program's by a relative error of at most 0.04.
Values may be sent and summed in bfloat16 or wider, within the bound.
No kernel may reach another device: no remote copies, remote signals or barrier semaphores. Data moves between devices by JAX's collectives and lax.ppermute only.
A program may use at most 320 MiB of HBM per device.

```python
import math
import jax
import jax.numpy as jnp
from jax import lax

D = 1024
HEADS = 16
HD = 64
FF = 4096
SEQ_DEV = 512
SEQ = 2048
TOKENS = 16384
N_DP = 8


def draw_lengths(key, part):
    key = jax.random.fold_in(key, 11)
    key_lengths, key_long, key_step = jax.random.split(key, 3)
    draws_all = jax.random.randint(key_lengths, (N_DP,), SEQ_DEV, SEQ + 1, dtype=jnp.int32)
    longest = jax.random.randint(key_long, (), 0, N_DP, dtype=jnp.int32)
    offset = jax.random.randint(key_step, (), 1, N_DP, dtype=jnp.int32)
    shortest = (longest + offset) % N_DP
    draws_all = draws_all.at[longest].set(SEQ)
    draws_all = draws_all.at[shortest].set(SEQ_DEV)
    return draws_all


def block_scale(own_key, shape, shards, smallest, top_value):
    factor_of, own = 1.0, jax.random.fold_in(own_key, 6)
    for dim, shards_of in shards:
        steps = jnp.exp(jax.random.uniform(jax.random.fold_in(own, dim), (shards_of,), jnp.float32, smallest / len(shards), top_value / len(shards)))
        factor_of = factor_of * jnp.repeat(steps, shape[dim] // shards_of).reshape([-1 if axis == dim else 1 for axis in range(len(shape))])
    return factor_of


def bell_draw(key, extent, width, bound, shards=(), kind=jnp.bfloat16):
    entries = jax.random.normal(key, extent, jnp.float32) * width
    if len(shards) > 0:
        entries = block_scale(key, extent, shards, -0.22, 0.18) * entries
    return jnp.clip(entries, min=-bound, max=bound).astype(kind)


def setup_inputs(seed: int = 0) -> dict:
    keys = jax.random.split(jax.random.key(seed), 19)
    tokens = bell_draw(keys[0], (TOKENS, D), 1.0, 6.0, ((0, 32),))
    lengths = draw_lengths(jax.random.fold_in(keys[18], 71), 0)
    cotangent = bell_draw(keys[2], (TOKENS, D), 1.0, 6.0, ((0, 32),))
    query_proj = bell_draw(keys[3], (D, D), (D // 4) ** -0.5, 0.375, ((0, 32),), jnp.float32)
    query_offset = bell_draw(keys[4], (D,), 0.3, 2.0, ((0, 32),), jnp.float32)
    key_proj = bell_draw(keys[5], (D, D), D ** -0.5, 0.1875, ((0, 32),), jnp.float32)
    value_proj = bell_draw(keys[6], (D, D), D ** -0.5, 0.1875, ((0, 32),), jnp.float32)
    value_offset = bell_draw(keys[7], (D,), 0.05, 0.3, ((0, 32),), jnp.float32)
    attn_proj = bell_draw(keys[8], (D, D), (D // 64) ** -0.5, 1.5, ((0, 32),), jnp.float32)
    attn_offset = bell_draw(keys[9], (D,), 0.3, 2.0, ((0, 32),), jnp.float32)
    attn_gain = jnp.clip(1.0 + 0.18 * jax.random.normal(keys[10], (D,), jnp.float32), 0.1, 1.9)
    attn_shift = bell_draw(keys[11], (D,), 0.3, 2.0, ((0, 32),), jnp.float32)
    inner_proj = bell_draw(keys[12], (D, FF), D ** -0.5, 0.1875, ((0, 32),), jnp.float32)
    inner_offset = bell_draw(keys[13], (FF,), 0.3, 2.0, ((0, 32),), jnp.float32)
    outer_proj = bell_draw(keys[14], (FF, D), FF ** -0.5, 0.09375, ((0, 32),), jnp.float32)
    outer_offset = bell_draw(keys[15], (D,), 0.3, 2.0, ((0, 32),), jnp.float32)
    final_gain = jnp.clip(1.0 + 0.18 * jax.random.normal(keys[16], (D,), jnp.float32), 0.1, 1.9)
    final_shift = bell_draw(keys[17], (D,), 0.3, 2.0, ((0, 32),), jnp.float32)
    return {"tokens": tokens, "lengths": lengths, "cotangent": cotangent, "query_proj": query_proj, "query_offset": query_offset, "key_proj": key_proj, "value_proj": value_proj, "value_offset": value_offset, "attn_proj": attn_proj, "attn_offset": attn_offset, "attn_gain": attn_gain, "attn_shift": attn_shift, "inner_proj": inner_proj, "inner_offset": inner_offset, "outer_proj": outer_proj, "outer_offset": outer_offset, "final_gain": final_gain, "final_shift": final_shift}


@jax.custom_vjp
def low(v):
    return lax.optimization_barrier(v.astype(jnp.bfloat16)).astype(jnp.float32)

@jax.custom_vjp
def low_back(v):
    return v

def low_keep(v):
    return (low(v), None)

def low_pass(kept, grad):
    return (grad,)

def back_keep(v):
    return (v, None)

def back_low(kept, grad):
    return (low(grad),)
low.defvjp(low_keep, low_pass)
low_back.defvjp(back_keep, back_low)
norm_eps = 1e-05

def round_both(value):
    return low(low_back(value))

def matmul(left, right):
    return jnp.dot(left, right, precision=lax.Precision.HIGHEST, preferred_element_type=jnp.float32)

def layer_norm(residual, norm_gain, norm_shift):
    centered = residual - lax.optimization_barrier(jnp.mean(residual, axis=1, keepdims=True))
    inverse = lax.rsqrt(lax.optimization_barrier(jnp.mean(centered * centered, axis=1, keepdims=True)) + norm_eps)
    return centered * inverse * norm_gain + norm_shift

def gelu_value(pre_act):
    return 0.5 * pre_act * (1.0 + lax.erf(pre_act * (1.0 / math.sqrt(2.0))))

def layer_sequence(seq_tokens, seq_length, params):
    w_query, b_query, w_key, w_value, b_value, w_attn, b_attn, g_attn, s_attn, w_inner, b_inner, w_outer, b_outer, g_final, s_final = params
    positions = jnp.arange(SEQ, dtype=jnp.int32)
    key_mask = positions < seq_length
    row_weight = key_mask.astype(jnp.float32)[:, None]
    queries = round_both(matmul(seq_tokens, w_query) + b_query)
    keys_seq = round_both(matmul(seq_tokens, w_key))
    values_seq = round_both(matmul(seq_tokens, w_value) + b_value)
    block_rows = min(SEQ, 512)
    score_scale = 1.0 / math.sqrt(HD)
    key_heads = keys_seq.reshape(SEQ, HEADS, HD)
    value_heads = values_seq.reshape(SEQ, HEADS, HD)

    def attend_block(query_block):
        query_heads = query_block.reshape(block_rows, HEADS, HD)
        raw_scores = jnp.einsum('qhd,khd->hqk', query_heads, key_heads, precision=lax.Precision.HIGHEST)
        scores = jnp.where(key_mask[None, None, :], low_back(raw_scores) * score_scale, -1e+30)
        row_top = lax.optimization_barrier(jnp.max(scores, axis=2, keepdims=True))
        shifted = jnp.where(key_mask[None, None, :], jnp.exp(scores - row_top), 0.0)
        log_total = row_top + jnp.log(lax.optimization_barrier(jnp.sum(shifted, axis=2, keepdims=True)))
        probs = jnp.where(key_mask[None, None, :], jnp.exp(scores - log_total), 0.0)
        mixed_heads = jnp.einsum('hqk,khd->qhd', low(probs), value_heads, precision=lax.Precision.HIGHEST)
        return mixed_heads.reshape(block_rows, HEADS * HD)
    mixed = lax.map(jax.checkpoint(attend_block), queries.reshape(SEQ // block_rows, block_rows, D))
    mixed_low = round_both(mixed.reshape(SEQ, D))
    attn_out = low_back(matmul(mixed_low, w_attn) + b_attn)
    hidden = layer_norm(seq_tokens + attn_out, g_attn, s_attn)
    pre_act = low_back(matmul(low(hidden), w_inner) + b_inner)
    outer = low_back(matmul(low(gelu_value(pre_act)), w_outer) + b_outer)
    return layer_norm(hidden + outer, g_final, s_final) * row_weight

def reference(tokens, lengths, cotangent, query_proj, query_offset, key_proj, value_proj, value_offset, attn_proj, attn_offset, attn_gain, attn_shift, inner_proj, inner_offset, outer_proj, outer_offset, final_gain, final_shift):
    masters = (query_proj, query_offset, key_proj, value_proj, value_offset, attn_proj, attn_offset, attn_gain, attn_shift, inner_proj, inner_offset, outer_proj, outer_offset, final_gain, final_shift)

    def forward(token_rows, master_list):
        params = tuple((low(item) for item in master_list))
        token_seqs = token_rows.reshape(N_DP, SEQ, D)

        def per_sequence(running, pieces):
            return (running, jax.checkpoint(layer_sequence)(pieces[0], pieces[1], params))
        running, outputs = lax.scan(per_sequence, jnp.zeros((), jnp.float32), (token_seqs, lengths))
        return outputs.reshape(N_DP * SEQ, D)
    layer_out, pullback = jax.vjp(forward, tokens.astype(jnp.float32), masters)
    token_grad, master_grads = pullback(cotangent.astype(jnp.float32))
    return (layer_out.astype(jnp.bfloat16), token_grad.astype(jnp.bfloat16), master_grads[0], master_grads[1], master_grads[2], master_grads[3], master_grads[4], master_grads[5], master_grads[6], master_grads[7], master_grads[8], master_grads[9], master_grads[10], master_grads[11], master_grads[12], master_grads[13], master_grads[14])
```

```python
import functools
import math

import jax
import jax.numpy as jnp
from jax import lax
from jax.experimental import pallas as pl
from jax.experimental.pallas import tpu as pltpu
from jax.sharding import PartitionSpec as P

HD = 64
AXES = ("dp", "ctx")
norm_eps = 1e-05
score_scale = 1.0 / math.sqrt(HD)
score_scale_two = score_scale * math.log2(math.e)
f32 = jnp.float32
bf16 = jnp.bfloat16


def attention_forward_kernel(
    length_ref, q_ref, k_ref, v_ref, mixed_ref, lse_ref, keys_t_ref, *, heads, rows
):
    width = k_ref.shape[1]
    seq = keys_t_ref.shape[1]

    @pl.when(pl.program_id(0) == 0)
    def _():
        keys_t_ref[...] = k_ref[...].T

    queries = q_ref[...]
    keys_t = keys_t_ref[...]
    values = v_ref[...]
    key_pos = lax.broadcasted_iota(jnp.int32, (1, seq), 1)
    bias = jnp.where(key_pos < length_ref[0], 0.0, -1e30).astype(f32)
    head_of = lax.broadcasted_iota(jnp.int32, (rows, width), 1) // HD
    lane = lax.broadcasted_iota(jnp.int32, (rows, 128), 1)
    mixed = jnp.zeros((rows, width), f32)
    lse = jnp.zeros((rows, 128), f32)
    for head in range(heads):
        own = jnp.where(head_of == head, queries, jnp.zeros_like(queries))
        scores = jnp.dot(own, keys_t, preferred_element_type=f32) * score_scale_two + bias
        top = jnp.max(scores, axis=1, keepdims=True)
        probs = jnp.exp2(scores - top)
        total = jnp.sum(probs, axis=1, keepdims=True)
        part = jnp.dot(probs.astype(bf16), values, preferred_element_type=f32)
        mixed = jnp.where(head_of == head, part * (1.0 / total), mixed)
        lse = jnp.where(lane == head, top + jnp.log2(total), lse)
    mixed_ref[...] = mixed.astype(bf16)
    lse_ref[...] = lse.T[:8]


def attention_forward(qkv, length, seq, rows=512):
    width = qkv.shape[1] // 3
    heads = width // HD
    return pl.pallas_call(
        functools.partial(attention_forward_kernel, heads=heads, rows=rows),
        grid=(seq // rows,),
        in_specs=[
            pl.BlockSpec(memory_space=pltpu.SMEM),
            pl.BlockSpec((rows, width), lambda i: (i, 0)),
            pl.BlockSpec((seq, width), lambda i: (0, 1)),
            pl.BlockSpec((seq, width), lambda i: (0, 2)),
        ],
        out_specs=[
            pl.BlockSpec((rows, width), lambda i: (i, 0)),
            pl.BlockSpec((8, rows), lambda i: (0, i)),
        ],
        out_shape=[
            jax.ShapeDtypeStruct((seq, width), bf16),
            jax.ShapeDtypeStruct((8, seq), f32),
        ],
        scratch_shapes=[pltpu.VMEM((width, seq), bf16)],
        compiler_params=pltpu.CompilerParams(vmem_limit_bytes=56 * 2**20),
        cost_estimate=pl.CostEstimate(
            flops=16 * seq * seq * width,
            bytes_accessed=8 * seq * width,
            transcendentals=seq * seq * heads,
        ),
        name="attention_forward",
    )(length, qkv, qkv, qkv)


def attention_backward_kernel(
    length_ref,
    q_ref,
    k_ref,
    v_ref,
    mixed_ref,
    dmixed_ref,
    lse_ref,
    dq_ref,
    dk_ref,
    dv_ref,
    keys_t_ref,
    dk_sum,
    dv_sum,
    *,
    heads,
    rows,
    depth,
):
    step = pl.program_id(0)
    seq, width = dk_sum.shape

    @pl.when(step == 0)
    def _():
        keys_t_ref[...] = k_ref[...].T
        dk_sum[...] = jnp.zeros_like(dk_sum)
        dv_sum[...] = jnp.zeros_like(dv_sum)

    queries, dmixed = q_ref[...], dmixed_ref[...]
    queries_t, dmixed_t, mixed_t = queries.T, dmixed.T, mixed_ref[...].T
    product = dmixed_t.astype(f32) * mixed_t.astype(f32)
    lane_head = lax.broadcasted_iota(jnp.int32, (rows, width), 1) // HD
    row_head = lax.broadcasted_iota(jnp.int32, (width, rows), 0) // HD
    none, none_t = jnp.zeros_like(queries), jnp.zeros_like(queries_t)
    lse = lse_ref[...]
    per_head = []
    for head in range(heads):
        per_head.append(
            (
                jnp.where(row_head == head, queries_t, none_t),
                jnp.where(row_head == head, dmixed_t, none_t),
                jnp.where(lane_head == head, queries, none),
                jnp.where(lane_head == head, dmixed, none),
                jnp.sum(product[HD * head : HD * head + HD], axis=0, keepdims=True),
                lse[head : head + 1],
            )
        )
    length = length_ref[0]

    def chunk(index, dq_t):
        span = pl.ds(pl.multiple_of(index * depth, depth), depth)
        keys, values = k_ref[span, :], v_ref[span, :]
        key_pos = index * depth + lax.broadcasted_iota(jnp.int32, (depth, 1), 0)
        bias = jnp.where(key_pos < length, 0.0, -1e30).astype(f32)
        dk, dv = dk_sum[span, :], dv_sum[span, :]
        new_dq_t = []
        for head in range(heads):
            own_q_t, own_do_t, own_q, own_do, delta, own_lse = per_head[head]
            scores = jnp.dot(keys, own_q_t, preferred_element_type=f32)
            probs = jnp.exp2(scores * score_scale_two + bias - own_lse)
            dprobs = jnp.dot(values, own_do_t, preferred_element_type=f32)
            dscores = (probs * (dprobs - delta)).astype(bf16)
            dv = dv + jnp.dot(probs.astype(bf16), own_do, preferred_element_type=f32)
            dk = dk + jnp.dot(dscores, own_q, preferred_element_type=f32)
            own_keys_t = keys_t_ref[HD * head : HD * head + HD, span]
            new_dq_t.append(
                dq_t[head] + jnp.dot(own_keys_t, dscores, preferred_element_type=f32)
            )
        dk_sum[span, :] = dk
        dv_sum[span, :] = dv
        return tuple(new_dq_t)

    start = tuple(jnp.zeros((HD, rows), f32) for _ in range(heads))
    dq_t = jnp.concatenate(lax.fori_loop(0, seq // depth, chunk, start), axis=0)
    dq_ref[...] = (dq_t * score_scale).T.astype(bf16)

    @pl.when(step == pl.num_programs(0) - 1)
    def _():
        dk_ref[...] = (dk_sum[...] * score_scale).astype(bf16)
        dv_ref[...] = dv_sum[...].astype(bf16)


def attention_backward(qkv, mixed, dmixed, lse, length, rows=512, depth=512):
    seq, width = mixed.shape
    heads = width // HD
    block = pl.BlockSpec((rows, width), lambda i: (i, 0))
    whole = pl.BlockSpec((seq, width), lambda i: (0, 0))
    return pl.pallas_call(
        functools.partial(attention_backward_kernel, heads=heads, rows=rows, depth=depth),
        grid=(seq // rows,),
        in_specs=[
            pl.BlockSpec(memory_space=pltpu.SMEM),
            block,
            pl.BlockSpec((seq, width), lambda i: (0, 1)),
            pl.BlockSpec((seq, width), lambda i: (0, 2)),
            block,
            block,
            pl.BlockSpec((8, rows), lambda i: (0, i)),
        ],
        out_specs=[block, whole, whole],
        out_shape=[jax.ShapeDtypeStruct((seq, width), bf16)] * 3,
        scratch_shapes=[
            pltpu.VMEM((width, seq), bf16),
            pltpu.VMEM((seq, width), f32),
            pltpu.VMEM((seq, width), f32),
        ],
        compiler_params=pltpu.CompilerParams(vmem_limit_bytes=56 * 2**20),
        cost_estimate=pl.CostEstimate(
            flops=40 * seq * seq * width,
            bytes_accessed=16 * seq * width,
            transcendentals=seq * seq * heads,
        ),
        name="attention_backward",
    )(length, qkv, qkv, qkv, mixed, dmixed, lse)


def device_index():
    return lax.axis_index("dp") * lax.axis_size("ctx") + lax.axis_index("ctx")


def bits_of(count):
    return count.bit_length() - 1


def swap(values, bit):
    count = lax.axis_size("dp") * lax.axis_size("ctx")
    return lax.ppermute(values, AXES, [(i, i ^ (1 << bit)) for i in range(count)])


def own_bit(bit):
    return (device_index() >> bit) & 1


def scatter_step(terms, axis, bit, out_dtype=bf16):
    mine = own_bit(bit)
    received = swap(lax.dynamic_index_in_dim(terms, 1 - mine, axis, keepdims=False), bit)
    kept = lax.dynamic_index_in_dim(terms, mine, axis, keepdims=False)
    return (kept.astype(f32) + received.astype(f32)).astype(out_dtype)


def scatter_sum(terms, bit_order, out_dtype=bf16):
    left = sorted(bit_order, reverse=True)
    for turn, bit in enumerate(bit_order):
        last = turn == len(bit_order) - 1
        terms = scatter_step(terms, left.index(bit), bit, out_dtype if last else terms.dtype)
        left.remove(bit)
    return terms


def gather_dp(shard):
    low = bits_of(lax.axis_size("ctx"))
    high = low + bits_of(lax.axis_size("dp"))
    for turn, bit in enumerate(range(high - 1, low - 1, -1)):
        other = swap(shard, bit)
        shard = jnp.where(
            own_bit(bit) == 1,
            jnp.stack([other, shard], axis=turn),
            jnp.stack([shard, other], axis=turn),
        )
    return shard.reshape((lax.axis_size("dp"),) + shard.shape[high - low :])


def gather_line(block):
    count = lax.axis_size("ctx")
    place = lax.axis_index("ctx")
    held = jnp.zeros((count + 1,) + block.shape, block.dtype)
    held = lax.dynamic_update_index_in_dim(held, block, place, 0)
    from_left = from_right = block
    for step in range(1, count):
        from_left = lax.ppermute(from_left, "ctx", [(i, i + 1) for i in range(count - 1)])
        from_right = lax.ppermute(from_right, "ctx", [(i + 1, i) for i in range(count - 1)])
        left_slot = jnp.where(place >= step, place - step, count)
        right_slot = jnp.where(place + step < count, place + step, count)
        held = lax.dynamic_update_index_in_dim(held, from_left, left_slot, 0)
        held = lax.dynamic_update_index_in_dim(held, from_right, right_slot, 0)
    return held.reshape(((count + 1) * block.shape[0],) + block.shape[1:])


def layer_norm(residual, norm_gain, norm_shift):
    centered = residual - jnp.mean(residual, axis=1, keepdims=True)
    inverse = lax.rsqrt(jnp.mean(centered * centered, axis=1, keepdims=True) + norm_eps)
    normed = centered * inverse
    return (normed * norm_gain + norm_shift, normed, inverse)


def layer_norm_back(upstream, normed, inverse, norm_gain):
    scaled = upstream * norm_gain
    first_mean = jnp.mean(scaled, axis=1, keepdims=True)
    second_mean = jnp.mean(scaled * normed, axis=1, keepdims=True)
    return inverse * (scaled - first_mean - normed * second_mean)


def gelu_value(pre_act):
    return 0.5 * pre_act * (1.0 + lax.erf(pre_act * (1.0 / math.sqrt(2.0))))


def gelu_slope(pre_act):
    normal_cdf = 0.5 * (1.0 + lax.erf(pre_act * (1.0 / math.sqrt(2.0))))
    return normal_cdf + pre_act * jnp.exp(-0.5 * pre_act * pre_act) * (
        1.0 / math.sqrt(2.0 * math.pi)
    )


def row_sum(values):
    return jnp.sum(values.astype(f32), axis=0)


def local(
    tokens,
    lengths,
    cotangent,
    query_proj,
    query_offset,
    key_proj,
    value_proj,
    value_offset,
    attn_proj,
    attn_offset,
    attn_gain,
    attn_shift,
    inner_proj,
    inner_offset,
    outer_proj,
    outer_offset,
    final_gain,
    final_shift,
):
    n_dp, n_ctx = lax.axis_size("dp"), lax.axis_size("ctx")
    n_dev = n_dp * n_ctx
    dev_bits = bits_of(n_dev)
    ctx_bits = bits_of(n_ctx)
    rows, width = tokens.shape
    seq = rows * n_ctx
    group = width // n_ctx
    part = width // n_dev
    hidden_width = inner_proj.shape[1]
    hidden_part = hidden_width // n_dev
    columns = hidden_width // width
    place = lax.axis_index("ctx")

    vectors = jnp.concatenate(
        [
            query_offset,
            value_offset,
            attn_offset,
            attn_gain,
            attn_shift,
            outer_offset,
            final_gain,
            final_shift,
            inner_offset,
        ]
    ).astype(bf16)
    triple = jnp.stack([query_proj, key_proj, value_proj], axis=1).astype(bf16)
    by_group = triple.reshape(part, 3, n_ctx, group).transpose(2, 0, 1, 3)
    by_group = by_group.reshape(n_ctx, part, 3 * group)
    vector_rows = -(-vectors.shape[0] // (3 * group))
    vectors = jnp.pad(vectors, (0, vector_rows * 3 * group - vectors.shape[0]))
    vectors = vectors.reshape(vector_rows, 3 * group)
    vectors = jnp.pad(vectors, ((0, 16 - vector_rows), (0, 0)))
    packed = jnp.concatenate(
        [by_group, jnp.broadcast_to(vectors[None], (n_ctx,) + vectors.shape)], axis=1
    )
    packed = gather_dp(lax.all_to_all(packed, "ctx", 0, 0, tiled=True))
    w_group = packed[:, :, :part].reshape(width, 3 * group)
    vectors = packed[:, :, part : part + vector_rows].reshape(n_dev, -1)
    names = [vectors[:, i * part : (i + 1) * part].reshape(width).astype(f32) for i in range(8)]
    b_query, b_value, b_attn, g_attn, s_attn, b_outer, g_final, s_final = names
    b_inner = vectors[:, 8 * part : 8 * part + hidden_part].reshape(hidden_width).astype(f32)

    inner_rows = [
        inner_proj[:, j * width : (j + 1) * width] for j in range(columns)
    ]
    shard = jnp.concatenate([attn_proj] + inner_rows + [outer_proj], axis=0).astype(bf16)
    gathered = lax.all_gather(shard, AXES, axis=0, tiled=False)
    w_attn = gathered[:, :part].reshape(width, width)
    w_inner = jnp.concatenate(
        [
            gathered[:, part * (1 + j) : part * (2 + j)].reshape(width, width)
            for j in range(columns)
        ],
        axis=1,
    )
    w_outer = gathered[:, part * (1 + columns) :].reshape(hidden_width, width)

    tokens_all = gather_line(tokens)
    b_group = lax.dynamic_slice_in_dim(
        jnp.stack([b_query, jnp.zeros_like(b_query), b_value]), place * group, group, 1
    ).reshape(3 * group)
    qkv = (jnp.dot(tokens_all, w_group, preferred_element_type=f32) + b_group).astype(bf16)
    mixed_group, lse = attention_forward(qkv, lengths, seq)
    mixed = lax.all_to_all(mixed_group.reshape(n_ctx, rows, group), "ctx", 0, 0, tiled=True)
    mixed = mixed.transpose(1, 0, 2).reshape(rows, width)

    row_valid = place * rows + jnp.arange(rows, dtype=jnp.int32) < lengths[0]
    row_weight = row_valid.astype(f32)[:, None]
    first_res = (
        tokens.astype(f32) + jnp.dot(mixed, w_attn, preferred_element_type=f32) + b_attn
    )
    hidden, normed_one, inverse_one = layer_norm(first_res, g_attn, s_attn)
    hidden_low = hidden.astype(bf16)
    pre_act = jnp.dot(hidden_low, w_inner, preferred_element_type=f32) + b_inner
    activated = gelu_value(pre_act).astype(bf16)
    second_res = hidden + jnp.dot(activated, w_outer, preferred_element_type=f32) + b_outer
    final, normed_two, inverse_two = layer_norm(second_res, g_final, s_final)
    layer_out = (final * row_weight).astype(bf16)

    upstream = cotangent.astype(f32) * row_weight
    grad_final_shift = jnp.sum(upstream, axis=0)
    grad_final_gain = jnp.sum(upstream * normed_two, axis=0)
    dsecond = layer_norm_back(upstream, normed_two, inverse_two, g_final)
    douter = dsecond.astype(bf16)
    grad_outer_offset = row_sum(douter)
    dactivated = jnp.einsum("sd,fd->sf", douter, w_outer, preferred_element_type=f32)
    dpre_act = (dactivated * gelu_slope(pre_act)).astype(bf16)
    grad_inner_offset = row_sum(dpre_act)
    dhidden = dsecond + jnp.einsum("sf,df->sd", dpre_act, w_inner, preferred_element_type=f32)
    grad_attn_shift = jnp.sum(dhidden, axis=0)
    grad_attn_gain = jnp.sum(dhidden * normed_one, axis=0)
    dfirst = layer_norm_back(dhidden, normed_one, inverse_one, g_attn)
    dattn = dfirst.astype(bf16)
    grad_attn_offset = row_sum(dattn)
    dmixed = jnp.einsum("se,de->sd", dattn, w_attn, preferred_element_type=f32).astype(bf16)

    dmixed_group = lax.all_to_all(
        dmixed.reshape(rows, n_ctx, group).transpose(1, 0, 2), "ctx", 0, 0, tiled=True
    ).reshape(seq, group)

    bits = (2,) * dev_bits
    order = list(range(ctx_bits, dev_bits)) + list(range(ctx_bits))
    swapped = order[:]
    if len(order) > 2 and dev_bits - ctx_bits > 2:
        swapped[1], swapped[2] = swapped[2], swapped[1]
    grad_outer = jnp.einsum("sf,sd->fd", activated, douter, preferred_element_type=f32)
    grad_outer = scatter_sum(
        grad_outer.astype(bf16).reshape(bits + (hidden_part, width)), order, f32
    )
    grad_inner = jnp.einsum("sd,sf->df", hidden_low, dpre_act, preferred_element_type=f32)
    grad_inner = scatter_sum(
        grad_inner.astype(bf16).reshape(bits + (part, hidden_width)), swapped, f32
    )
    grad_attn = jnp.einsum("sd,se->de", mixed, dattn, preferred_element_type=f32)
    grad_attn = scatter_sum(grad_attn.astype(bf16).reshape(bits + (part, width)), order, f32)
    early = [
        grad_attn_offset,
        grad_attn_gain,
        grad_attn_shift,
        grad_outer_offset,
        grad_final_gain,
        grad_final_shift,
        grad_inner_offset,
    ]
    early = jnp.concatenate([v.reshape(n_dev, -1) for v in early], axis=1)
    early = scatter_sum(early.reshape(bits + (1, early.shape[1])), order, f32).reshape(-1)

    dq, dk, dv = attention_backward(qkv, mixed_group, dmixed_group, lse, lengths)
    dqkv = jnp.concatenate([dq, dk, dv], axis=1)
    grad_triple = jnp.einsum(
        "sd,se->de", tokens_all[:seq], dqkv, preferred_element_type=f32
    ).astype(bf16)
    dp_order = order[: dev_bits - ctx_bits]
    grad_triple = grad_triple.reshape((2,) * len(dp_order) + (n_ctx * part, 3 * group))
    left = sorted(dp_order, reverse=True)
    for bit in dp_order:
        grad_triple = scatter_step(grad_triple, left.index(bit), bit)
        left.remove(bit)
    grad_triple = lax.all_to_all(
        grad_triple.reshape(n_ctx, part, 3 * group), "ctx", 0, 0, tiled=True
    )
    grad_triple = grad_triple.reshape(n_ctx, part, 3, group).transpose(2, 1, 0, 3)
    grad_triple = grad_triple.reshape(3, part, width).astype(f32)
    late = jnp.stack([row_sum(dq), row_sum(dv)])
    late = lax.dynamic_update_slice_in_dim(
        jnp.zeros((2, width), f32), late, place * group, 1
    )
    late = late.reshape(2, n_dev, part).transpose(1, 0, 2).reshape(bits + (1, 2 * part))
    late = scatter_sum(late, order, f32).reshape(2, part)

    dqkv_rows = lax.all_to_all(dqkv.reshape(n_ctx, rows, 3 * group), "ctx", 0, 0, tiled=True)
    w_triple = lax.all_gather(
        by_group.transpose(1, 0, 2).reshape(part, 3 * width), AXES, axis=0, tiled=True
    )
    dqkv_rows = dqkv_rows.transpose(1, 0, 2).reshape(rows, 3 * width)
    input_grad = (
        dfirst + jnp.einsum("se,de->sd", dqkv_rows, w_triple, preferred_element_type=f32)
    ).astype(bf16)

    pieces = [early[i * part : (i + 1) * part] for i in range(6)]
    return (
        layer_out,
        input_grad,
        grad_triple[0],
        late[0],
        grad_triple[1],
        grad_triple[2],
        late[1],
        grad_attn,
        pieces[0],
        pieces[1],
        pieces[2],
        grad_inner,
        early[6 * part :],
        grad_outer,
        pieces[3],
        pieces[4],
        pieces[5],
    )


def solution(mesh):
    rows, vector = P(AXES, None), P(AXES)
    in_specs = (rows, P("dp"), rows, rows, vector, rows, rows, vector, rows) + (vector,) * 3
    in_specs += (rows, vector, rows) + (vector,) * 3
    out_specs = (rows,) * 3 + (vector, rows, rows, vector, rows) + (vector,) * 3
    out_specs += (rows, vector, rows) + (vector,) * 3
    return jax.shard_map(local, mesh=mesh, in_specs=in_specs, out_specs=out_specs, check_vma=False)
```

```python
import functools
import math

import jax
import jax.numpy as jnp
from jax import lax
from jax.experimental import pallas as pl
from jax.experimental.pallas import tpu as pltpu
from jax.sharding import PartitionSpec as P

HD = 64
AXES = ("dp", "ctx")
norm_eps = 1e-05
score_scale = 1.0 / math.sqrt(HD)
score_scale_two = score_scale * math.log2(math.e)
f32 = jnp.float32
bf16 = jnp.bfloat16


def kernel_cost(flops):
    return flops // 8


def attention_forward_kernel(
    place_ref, q_ref, k_ref, v_ref, mixed_ref, lse_ref, keys_t_ref, *, heads, rows
):
    width = k_ref.shape[1]
    seq = keys_t_ref.shape[1]

    @pl.when(pl.program_id(0) == 0)
    def _():
        keys_t_ref[...] = k_ref[...].T

    queries = q_ref[...]
    keys_t = keys_t_ref[...]
    values = v_ref[...]
    slots = [
        (place_ref[0] ^ slot) * rows + lax.broadcasted_iota(jnp.int32, (1, rows), 1)
        for slot in range(seq // rows)
    ]
    key_pos = jnp.concatenate(slots, axis=1)
    bias = jnp.where(key_pos < place_ref[1], 0.0, -1e30).astype(f32)
    head_of = lax.broadcasted_iota(jnp.int32, (rows, width), 1) // HD
    lane = lax.broadcasted_iota(jnp.int32, (rows, 128), 1)
    mixed = jnp.zeros((rows, width), f32)
    lse = jnp.zeros((rows, 128), f32)
    for head in range(heads):
        own = jnp.where(head_of == head, queries, jnp.zeros_like(queries))
        scores = jnp.dot(own, keys_t, preferred_element_type=f32) * score_scale_two + bias
        top = jnp.max(scores, axis=1, keepdims=True)
        probs = jnp.exp2(scores - top)
        total = jnp.sum(probs, axis=1, keepdims=True)
        part = jnp.dot(probs.astype(bf16), values, preferred_element_type=f32)
        mixed = jnp.where(head_of == head, part * (1.0 / total), mixed)
        lse = jnp.where(lane == head, top + jnp.log2(total), lse)
    mixed_ref[...] = mixed.astype(bf16)
    lse_ref[...] = lse.T[:8]


def attention_forward(qkv, place, rows, chunk, chunks):
    seq = qkv.shape[0]
    width = qkv.shape[1] // (3 * chunks)
    heads = width // HD
    return pl.pallas_call(
        functools.partial(attention_forward_kernel, heads=heads, rows=rows),
        grid=(seq // rows,),
        in_specs=[
            pl.BlockSpec(memory_space=pltpu.SMEM),
            pl.BlockSpec((rows, width), lambda i: (i, chunk)),
            pl.BlockSpec((seq, width), lambda i: (0, chunks + chunk)),
            pl.BlockSpec((seq, width), lambda i: (0, 2 * chunks + chunk)),
        ],
        out_specs=[
            pl.BlockSpec((rows, width), lambda i: (i, 0)),
            pl.BlockSpec((8, rows), lambda i: (0, i)),
        ],
        out_shape=[
            jax.ShapeDtypeStruct((seq, width), bf16),
            jax.ShapeDtypeStruct((8, seq), f32),
        ],
        scratch_shapes=[pltpu.VMEM((width, seq), bf16)],
        compiler_params=pltpu.CompilerParams(vmem_limit_bytes=56 * 2**20),
        cost_estimate=pl.CostEstimate(
            flops=kernel_cost(16 * seq * seq * width),
            bytes_accessed=8 * seq * width,
            transcendentals=seq * seq * heads,
        ),
        name="attention_forward",
    )(place, qkv, qkv, qkv)


def attention_backward_kernel(
    place_ref,
    q_ref,
    k_ref,
    v_ref,
    mixed_ref,
    lse_ref,
    *refs,
    heads,
    rows,
):
    step = pl.program_id(0)
    dmixed_refs, (out_ref, keys_t_ref, dk_sum, dv_sum, dmixed_ref) = refs[:-5], refs[-5:]
    seq, width = dk_sum.shape
    for slot, slot_ref in enumerate(dmixed_refs):

        @pl.when(step == slot)
        def _(slot_ref=slot_ref):
            dmixed_ref[...] = slot_ref[...]

    @pl.when(step == 0)
    def _():
        keys_t_ref[...] = k_ref[...].T
        dk_sum[...] = jnp.zeros_like(dk_sum)
        dv_sum[...] = jnp.zeros_like(dv_sum)

    queries, dmixed = q_ref[...], dmixed_ref[...]
    queries_t, dmixed_t, mixed_t = queries.T, dmixed.T, mixed_ref[...].T
    product = dmixed_t.astype(f32) * mixed_t.astype(f32)
    lane_head = lax.broadcasted_iota(jnp.int32, (rows, width), 1) // HD
    row_head = lax.broadcasted_iota(jnp.int32, (width, rows), 0) // HD
    none, none_t = jnp.zeros_like(queries), jnp.zeros_like(queries_t)
    lse = lse_ref[...]
    per_head = []
    for head in range(heads):
        per_head.append(
            (
                jnp.where(row_head == head, queries_t, none_t),
                jnp.where(row_head == head, dmixed_t, none_t),
                jnp.where(lane_head == head, queries, none),
                jnp.where(lane_head == head, dmixed, none),
                jnp.sum(product[HD * head : HD * head + HD], axis=0, keepdims=True),
                lse[head : head + 1],
            )
        )

    def chunk(index, dq_t):
        span = pl.ds(pl.multiple_of(index * rows, rows), rows)
        keys, values = k_ref[span, :], v_ref[span, :]
        key_pos = (place_ref[0] ^ index) * rows + lax.broadcasted_iota(jnp.int32, (rows, 1), 0)
        bias = jnp.where(key_pos < place_ref[1], 0.0, -1e30).astype(f32)
        dk, dv = dk_sum[span, :], dv_sum[span, :]
        new_dq_t = []
        for head in range(heads):
            own_q_t, own_do_t, own_q, own_do, delta, own_lse = per_head[head]
            scores = jnp.dot(keys, own_q_t, preferred_element_type=f32)
            probs = jnp.exp2(scores * score_scale_two + bias - own_lse)
            dprobs = jnp.dot(values, own_do_t, preferred_element_type=f32)
            dscores = (probs * (dprobs - delta)).astype(bf16)
            dv = dv + jnp.dot(probs.astype(bf16), own_do, preferred_element_type=f32)
            dk = dk + jnp.dot(dscores, own_q, preferred_element_type=f32)
            own_keys_t = keys_t_ref[HD * head : HD * head + HD, span]
            new_dq_t.append(
                dq_t[head] + jnp.dot(own_keys_t, dscores, preferred_element_type=f32)
            )
        dk_sum[span, :] = dk
        dv_sum[span, :] = dv
        return tuple(new_dq_t)

    start = tuple(jnp.zeros((HD, rows), f32) for _ in range(heads))
    dq_t = jnp.concatenate(lax.fori_loop(0, seq // rows, chunk, start), axis=0)
    own_rows = pl.ds(pl.multiple_of(step * rows, rows), rows)
    out_ref[own_rows, :width] = (dq_t * score_scale).T.astype(bf16)

    @pl.when(step == pl.num_programs(0) - 1)
    def _():
        out_ref[:, width : 2 * width] = (dk_sum[...] * score_scale).astype(bf16)
        out_ref[:, 2 * width :] = dv_sum[...].astype(bf16)


def attention_backward(qkv, mixed, dmixed_slots, lse, place, chunk, chunks):
    seq, width = mixed.shape
    rows = seq // len(dmixed_slots)
    heads = width // HD
    block = pl.BlockSpec((rows, width), lambda i: (i, 0))
    return pl.pallas_call(
        functools.partial(attention_backward_kernel, heads=heads, rows=rows),
        grid=(seq // rows,),
        in_specs=[
            pl.BlockSpec(memory_space=pltpu.SMEM),
            pl.BlockSpec((rows, width), lambda i: (i, chunk)),
            pl.BlockSpec((seq, width), lambda i: (0, chunks + chunk)),
            pl.BlockSpec((seq, width), lambda i: (0, 2 * chunks + chunk)),
            block,
            pl.BlockSpec((8, rows), lambda i: (0, i)),
        ]
        + [pl.BlockSpec((rows, width), lambda i: (0, chunk))] * len(dmixed_slots),
        out_specs=pl.BlockSpec((seq, 3 * width), lambda i: (0, 0)),
        out_shape=jax.ShapeDtypeStruct((seq, 3 * width), bf16),
        scratch_shapes=[
            pltpu.VMEM((width, seq), bf16),
            pltpu.VMEM((seq, width), f32),
            pltpu.VMEM((seq, width), f32),
            pltpu.VMEM((rows, width), bf16),
        ],
        compiler_params=pltpu.CompilerParams(vmem_limit_bytes=56 * 2**20),
        cost_estimate=pl.CostEstimate(
            flops=kernel_cost(40 * seq * seq * width),
            bytes_accessed=16 * seq * width,
            transcendentals=seq * seq * heads,
        ),
        name="attention_backward",
    )(place, qkv, qkv, qkv, mixed, lse, *dmixed_slots)


def layer_kernel(
    place_ref,
    tokens_ref,
    cotangent_ref,
    vectors_ref,
    inner_offset_ref,
    *refs,
    chunks,
    groups,
):
    mixed_refs, refs = refs[: chunks * groups], refs[chunks * groups :]
    weight_refs, refs = refs[:2], refs[2:]
    (layer_out_ref, dfirst_ref, sums_ref, inner_sum_ref), refs = refs[:4], refs[4:]
    dmixed_refs, gradient_refs, refs = refs[:groups], refs[groups : groups + 6], refs[groups + 6 :]
    (w_attn, w_inner, w_outer), refs = refs[:3], refs[3:]
    (mixed_ref, hidden_ref, act_ref, douter_ref, dpre_ref, dattn_ref), refs = refs[:6], refs[6:]
    (wide_ref, normed_ref, inverse_ref, total_ref, dmixed_ref, turned_ref, sems) = refs
    rows, width = tokens_ref.shape
    hidden_width = w_inner.shape[1]
    place, length, core, quad = place_ref[0], place_ref[1], place_ref[2], place_ref[3]
    first_row = place * rows

    first_weights, outer_weights = weight_refs
    copies = [
        pltpu.make_async_copy(first_weights.at[:, :width], w_attn, sems.at[0]),
        pltpu.make_async_copy(first_weights.at[:, width:], w_inner, sems.at[1]),
        pltpu.make_async_copy(outer_weights, w_outer, sems.at[2]),
    ]
    for copy in copies:
        copy.start()

    b_attn, g_attn, s_attn = vectors_ref[0:1], vectors_ref[1:2], vectors_ref[2:3]
    b_outer, g_final, s_final = vectors_ref[3:4], vectors_ref[4:5], vectors_ref[5:6]
    chunk_width = mixed_refs[0].shape[1]

    def columns_of(chunk, slot):
        start = ((place ^ slot) * chunks + chunk) * chunk_width
        return pl.ds(pl.multiple_of(start, chunk_width), chunk_width)

    for chunk in range(chunks):
        for slot in range(groups):
            mixed_ref[:, columns_of(chunk, slot)] = mixed_refs[chunk * groups + slot][...]

    copies[0].wait()

    step = 128

    def norm_one(turn, carried):
        span = pl.ds(pl.multiple_of(turn * step, step), step)
        first = (
            tokens_ref[span, :].astype(f32)
            + jnp.dot(mixed_ref[span, :], w_attn[...], preferred_element_type=f32)
            + b_attn
        )
        centered = first - jnp.mean(first, axis=1, keepdims=True)
        inverse = lax.rsqrt(jnp.mean(centered * centered, axis=1, keepdims=True) + norm_eps)
        normed = centered * inverse
        hidden = normed * g_attn + s_attn
        normed_ref[span, :] = normed
        inverse_ref[span, :] = jnp.broadcast_to(inverse, (step, 128))
        total_ref[span, :] = hidden
        hidden_ref[span, :] = hidden.astype(bf16)
        return carried

    lax.fori_loop(0, rows // step, norm_one, 0)

    copies[1].wait()
    block = 512

    def feed_in(turn, carried):
        span = pl.ds(pl.multiple_of(turn * block, block), block)
        pre = (
            jnp.dot(hidden_ref[...], w_inner[:, span], preferred_element_type=f32)
            + inner_offset_ref[:, span]
        )
        normal_cdf = 0.5 * (1.0 + lax.erf(pre * (1.0 / math.sqrt(2.0))))
        act_ref[:, span] = (pre * normal_cdf).astype(bf16)
        slope = normal_cdf + pre * jnp.exp(-0.5 * pre * pre) * (1.0 / math.sqrt(2.0 * math.pi))
        dpre_ref[:, span] = slope.astype(bf16)
        return carried

    lax.fori_loop(0, hidden_width // block, feed_in, 0)

    copies[2].wait()
    narrow = 512

    def feed_out(turn, carried):
        span = pl.ds(pl.multiple_of(turn * narrow, narrow), narrow)
        wide_ref[:, span] = jnp.dot(act_ref[...], w_outer[:, span], preferred_element_type=f32)
        return carried

    lax.fori_loop(0, width // narrow, feed_out, 0)

    def norm_two(turn, carried):
        span = pl.ds(pl.multiple_of(turn * step, step), step)
        second = total_ref[span, :] + wide_ref[span, :] + b_outer
        centered = second - jnp.mean(second, axis=1, keepdims=True)
        inverse = lax.rsqrt(jnp.mean(centered * centered, axis=1, keepdims=True) + norm_eps)
        normed = centered * inverse
        row = first_row + turn * step + lax.broadcasted_iota(jnp.int32, (step, 1), 0)
        valid = jnp.where(row < length, 1.0, 0.0).astype(f32)
        layer_out_ref[span, :] = ((normed * g_final + s_final) * valid).astype(bf16)
        upstream = cotangent_ref[span, :].astype(f32) * valid
        shift_sum, gain_sum, offset_sum = carried
        shift_sum = shift_sum + jnp.sum(upstream, axis=0, keepdims=True)
        gain_sum = gain_sum + jnp.sum(upstream * normed, axis=0, keepdims=True)
        scaled = upstream * g_final
        first_mean = jnp.mean(scaled, axis=1, keepdims=True)
        second_mean = jnp.mean(scaled * normed, axis=1, keepdims=True)
        dsecond = inverse * (scaled - first_mean - normed * second_mean)
        total_ref[span, :] = dsecond
        douter = dsecond.astype(bf16)
        douter_ref[span, :] = douter
        offset_sum = offset_sum + jnp.sum(douter.astype(f32), axis=0, keepdims=True)
        return (shift_sum, gain_sum, offset_sum)

    none = jnp.zeros((1, width), f32)
    shift_sum, gain_sum, offset_sum = lax.fori_loop(
        0, rows // step, norm_two, (none, none, none)
    )
    sums_ref[0:1] = offset_sum
    sums_ref[1:2] = gain_sum
    sums_ref[2:3] = shift_sum

    across = (((1,), (1,)), ((), ()))

    def back_out(turn, carried):
        span = pl.ds(pl.multiple_of(turn * block, block), block)
        dact = lax.dot_general(
            douter_ref[...], w_outer[span, :], across, preferred_element_type=f32
        )
        dpre = (dact * dpre_ref[:, span].astype(f32)).astype(bf16)
        dpre_ref[:, span] = dpre
        inner_sum_ref[:, span] = jnp.sum(dpre.astype(f32), axis=0, keepdims=True)
        return carried

    lax.fori_loop(0, hidden_width // block, back_out, 0)

    quads = gradient_refs[0].shape[0]
    slab, outer_slab = width // (2 * quads), hidden_width // (2 * quads)
    left_width = gradient_refs[0].shape[2]
    down = (((0,), (0,)), ((), ()))

    def leave(first_sem, plan, height):
        started = []
        for source, from_col, cols, which, to_col in plan:
            for side in range(2):
                owner = 1 - core if side == 0 else core
                for slot in range(quads):
                    row = pl.multiple_of((2 * (slot ^ quad) + owner) * height, height)
                    copy = pltpu.make_async_copy(
                        source.at[pl.ds(row, height), from_col : from_col + cols],
                        gradient_refs[2 * which + side].at[slot, :, to_col : to_col + cols],
                        sems.at[first_sem + len(started)],
                    )
                    copy.start()
                    started.append(copy)
        return started

    def outer_gradient(turn, carried):
        span = pl.ds(pl.multiple_of(turn * block, block), block)
        terms = lax.dot_general(
            act_ref[:, span], douter_ref[...], down, preferred_element_type=f32
        )
        w_outer[span, :] = terms.astype(bf16)
        return carried

    lax.fori_loop(0, hidden_width // block, outer_gradient, 0)
    leaving = leave(3, ((w_outer, 0, width, 2, 0),), outer_slab)

    def back_in(turn, carried):
        span = pl.ds(pl.multiple_of(turn * narrow, narrow), narrow)
        wide_ref[:, span] = lax.dot_general(
            dpre_ref[...], w_inner[span, :], across, preferred_element_type=f32
        )
        return carried

    lax.fori_loop(0, width // narrow, back_in, 0)

    def norm_one_back(turn, carried):
        span = pl.ds(pl.multiple_of(turn * step, step), step)
        dhidden = total_ref[span, :] + wide_ref[span, :]
        normed = normed_ref[span, :]
        inverse = inverse_ref[span, 0:1]
        shift_sum, gain_sum, offset_sum = carried
        shift_sum = shift_sum + jnp.sum(dhidden, axis=0, keepdims=True)
        gain_sum = gain_sum + jnp.sum(dhidden * normed, axis=0, keepdims=True)
        scaled = dhidden * g_attn
        first_mean = jnp.mean(scaled, axis=1, keepdims=True)
        second_mean = jnp.mean(scaled * normed, axis=1, keepdims=True)
        dfirst = inverse * (scaled - first_mean - normed * second_mean)
        dfirst_ref[span, :] = dfirst
        dattn = dfirst.astype(bf16)
        dattn_ref[span, :] = dattn
        offset_sum = offset_sum + jnp.sum(dattn.astype(f32), axis=0, keepdims=True)
        dmixed = lax.dot_general(dattn, w_attn[...], across, preferred_element_type=f32)
        dmixed_ref[span, :] = dmixed.astype(bf16)
        return (shift_sum, gain_sum, offset_sum)

    shift_sum, gain_sum, offset_sum = lax.fori_loop(
        0, rows // step, norm_one_back, (none, none, none)
    )
    sums_ref[3:4] = offset_sum
    sums_ref[4:5] = gain_sum
    sums_ref[5:6] = shift_sum
    sums_ref[6:8] = jnp.zeros((2, width), f32)
    group_width = chunks * chunk_width
    for slot in range(groups):
        start = pl.multiple_of((place ^ slot) * group_width, group_width)
        dmixed_refs[slot][...] = dmixed_ref[:, pl.ds(start, group_width)]

    turned_ref[...] = hidden_ref[...].T
    wide_block = 1024

    def inner_gradient(turn, carried):
        span = pl.ds(pl.multiple_of(turn * wide_block, wide_block), wide_block)
        for half in range(width // block):
            rows_of = slice(half * block, (half + 1) * block)
            terms = jnp.dot(turned_ref[rows_of, :], dpre_ref[:, span], preferred_element_type=f32)
            w_inner[rows_of, span] = terms.astype(bf16)
        return carried

    lax.fori_loop(0, hidden_width // wide_block, inner_gradient, 0)
    leaving += leave(
        3 + len(leaving),
        (
            (w_inner, left_width - width, hidden_width + width - left_width, 1, 0),
            (w_inner, 0, left_width - width, 0, width),
        ),
        slab,
    )
    turned_ref[...] = mixed_ref[...].T
    for half in range(width // block):
        rows_of = slice(half * block, (half + 1) * block)
        terms = jnp.dot(turned_ref[rows_of, :], dattn_ref[...], preferred_element_type=f32)
        w_attn[rows_of, :] = terms.astype(bf16)
    leaving += leave(3 + len(leaving), ((w_attn, 0, width, 0, 0),), slab)
    for copy in leaving:
        copy.wait()


def layer_middle(place, tokens, cotangent, vectors, inner_offset, mixed_parts, groups, weights, quads):
    rows, width = tokens.shape
    hidden_width = inner_offset.shape[1]
    chunk_width = mixed_parts[0].shape[1]
    chunks = len(mixed_parts) // groups
    slab, outer_slab = width // (2 * quads), hidden_width // (2 * quads)
    left_width = 2 * width
    vmem = pl.BlockSpec(memory_space=pltpu.VMEM)
    anywhere = pl.BlockSpec(memory_space=pl.ANY)
    shapes = [
        jax.ShapeDtypeStruct((rows, width), bf16),
        jax.ShapeDtypeStruct((rows, width), f32),
        jax.ShapeDtypeStruct((8, width), f32),
        jax.ShapeDtypeStruct((1, hidden_width), f32),
    ] + [jax.ShapeDtypeStruct((rows, chunks * chunk_width), bf16)] * groups
    gradients = [
        jax.ShapeDtypeStruct((quads, slab, left_width), bf16),
        jax.ShapeDtypeStruct((quads, slab, width + hidden_width - left_width), bf16),
        jax.ShapeDtypeStruct((quads, outer_slab, width), bf16),
    ]
    gradients = [shape for shape in gradients for _ in range(2)]
    return pl.pallas_call(
        functools.partial(layer_kernel, chunks=chunks, groups=groups),
        in_specs=[pl.BlockSpec(memory_space=pltpu.SMEM)]
        + [vmem] * (4 + chunks * groups)
        + [anywhere] * 2,
        out_specs=[vmem] * len(shapes) + [anywhere] * 6,
        out_shape=shapes + gradients,
        scratch_shapes=[
            pltpu.VMEM((width, width), bf16),
            pltpu.VMEM((width, hidden_width), bf16),
            pltpu.VMEM((hidden_width, width), bf16),
            pltpu.VMEM((rows, width), bf16),
            pltpu.VMEM((rows, width), bf16),
            pltpu.VMEM((rows, hidden_width), bf16),
            pltpu.VMEM((rows, width), bf16),
            pltpu.VMEM((rows, hidden_width), bf16),
            pltpu.VMEM((rows, width), bf16),
            pltpu.VMEM((rows, width), f32),
            pltpu.VMEM((rows, width), f32),
            pltpu.VMEM((rows, 128), f32),
            pltpu.VMEM((rows, width), f32),
            pltpu.VMEM((rows, width), bf16),
            pltpu.VMEM((width, rows), bf16),
            pltpu.SemaphoreType.DMA((3 + 8 * quads,)),
        ],
        compiler_params=pltpu.CompilerParams(vmem_limit_bytes=60 * 2**20),
        cost_estimate=pl.CostEstimate(
            flops=kernel_cost(12 * rows * width * (hidden_width + width)),
            bytes_accessed=4 * width * (2 * hidden_width + width) + 10 * rows * width,
            transcendentals=2 * rows * hidden_width,
        ),
        name="layer_middle",
    )(place, tokens, cotangent, vectors, inner_offset, *mixed_parts, *weights)


def input_kernel(place_ref, dfirst_ref, weights_ref, *refs, chunks, groups):
    parts, (out_ref, rows_ref) = refs[:-2], refs[-2:]
    cols = parts[0].shape[1]
    for chunk in range(chunks):
        for slot in range(groups):
            start = (chunk * groups + (place_ref[0] ^ slot)) * cols
            span = pl.ds(pl.multiple_of(start, cols), cols)
            rows_ref[:, span] = parts[chunk * groups + slot][...]
    block = 256

    def columns(turn, carried):
        span = pl.ds(pl.multiple_of(turn * block, block), block)
        terms = lax.dot_general(
            rows_ref[...],
            weights_ref[span, :],
            (((1,), (1,)), ((), ())),
            preferred_element_type=f32,
        )
        out_ref[:, span] = (dfirst_ref[:, span] + terms).astype(bf16)
        return carried

    lax.fori_loop(0, out_ref.shape[1] // block, columns, 0)


def input_gradient(place, dfirst, weights, parts, groups):
    rows, width = dfirst.shape
    vmem = pl.BlockSpec(memory_space=pltpu.VMEM)
    return pl.pallas_call(
        functools.partial(input_kernel, chunks=len(parts) // groups, groups=groups),
        in_specs=[pl.BlockSpec(memory_space=pltpu.SMEM)] + [vmem] * (2 + len(parts)),
        out_specs=vmem,
        out_shape=jax.ShapeDtypeStruct((rows, width), bf16),
        scratch_shapes=[pltpu.VMEM((rows, weights.shape[1]), bf16)],
        compiler_params=pltpu.CompilerParams(vmem_limit_bytes=48 * 2**20),
        cost_estimate=pl.CostEstimate(
            flops=kernel_cost(2 * rows * width * weights.shape[1]),
            bytes_accessed=2 * width * weights.shape[1] + 12 * rows * width,
            transcendentals=0,
        ),
        name="input_gradient",
    )(place, dfirst, weights, *parts)


def device_index():
    return lax.axis_index("dp") * lax.axis_size("ctx") + lax.axis_index("ctx")


def bits_of(count):
    return count.bit_length() - 1


def swap(values, bit):
    count = lax.axis_size("dp") * lax.axis_size("ctx")
    return lax.ppermute(values, AXES, [(i, i ^ (1 << bit)) for i in range(count)])


def own_bit(bit):
    return (device_index() >> bit) & 1


def joined(shard, other, bit, axis):
    return jnp.where(
        own_bit(bit) == 1,
        jnp.stack([other, shard], axis=axis),
        jnp.stack([shard, other], axis=axis),
    )


def after(value, *others):
    return lax.optimization_barrier((value,) + others)[0]


def gather_line(block):
    count = lax.axis_size("ctx")
    place = lax.axis_index("ctx")
    held = jnp.broadcast_to(block[None], (count,) + block.shape)
    from_left = from_right = block
    for step in range(1, count):
        from_left, from_right = yield [
            lax.ppermute(from_left, "ctx", [(i, i + 1) for i in range(count - 1)]),
            lax.ppermute(from_right, "ctx", [(i + 1, i) for i in range(count - 1)]),
        ]
        for arrived, source in ((from_left, place - step), (from_right, place + step)):
            inside = (source >= 0) & (source < count)
            held = lax.dynamic_update_index_in_dim(
                held,
                jnp.where(inside, arrived, block),
                jnp.where(inside, source ^ place, 0),
                0,
            )
    return held.reshape((count * block.shape[0],) + block.shape[1:])


def exchange_slots(slots):
    count = lax.axis_size("ctx")
    return [slots[0]] + [
        lax.ppermute(slots[mask], "ctx", [(i, i ^ mask) for i in range(count)])
        for mask in range(1, count)
    ]


def exchange_line(blocks):
    count = lax.axis_size("ctx")
    place = lax.axis_index("ctx")
    arrived = yield [
        lax.ppermute(
            lax.dynamic_index_in_dim(blocks, place ^ mask, 0, keepdims=False),
            "ctx",
            [(i, i ^ mask) for i in range(count)],
        )
        for mask in range(1, count)
    ]
    for mask, value in enumerate(arrived, 1):
        blocks = lax.dynamic_update_index_in_dim(blocks, value, place ^ mask, 0)
    return blocks


def gather_bits(shard, bit_order):
    held = []
    for bit in bit_order:
        (other,) = yield [swap(shard, bit)]
        held = sorted(held + [bit], reverse=True)
        shard = joined(shard, other, bit, held.index(bit))
    return shard.reshape((2 ** len(held),) + shard.shape[len(held) :])


def gather_group(packed, bit_order):
    packed = yield from exchange_line(packed)
    return (yield from gather_bits(packed, bit_order))


def scatter_sum(parts, bit_order, out_dtype, sent):
    left = sorted(bit_order, reverse=True)
    for bit in bit_order:
        axis, mine = left.index(bit), own_bit(bit)
        if bit >= bits_of(lax.axis_size("ctx")):
            given = [lax.index_in_dim(part, 1, axis, keepdims=False) for part in parts]
            parts = [lax.index_in_dim(part, 0, axis, keepdims=False) for part in parts]
        else:
            given = [lax.dynamic_index_in_dim(part, 1 - mine, axis, False) for part in parts]
            parts = [lax.dynamic_index_in_dim(part, mine, axis, False) for part in parts]
        given = total_of(given, parts[0].dtype)
        sent.append(given)
        parts = parts + (yield [swap(given, bit)])
        left.remove(bit)
    return total_of(parts, out_dtype)


def total_of(parts, dtype):
    total = parts[0].astype(f32)
    for part in parts[1:]:
        total = total + part.astype(f32)
    return total.astype(dtype)


def scatter_core(terms, bit):
    mine = own_bit(bit)
    (received,) = yield [swap(lax.dynamic_index_in_dim(terms, 1 - mine, 1, False), bit)]
    kept = lax.dynamic_index_in_dim(terms, mine, 1, False)
    return total_of([kept, received], terms.dtype)


def scatter_at_once(terms, bits):
    masks = range(1, 2 ** len(bits))
    low = min(bits)
    place = (device_index() >> low) & (2 ** len(bits) - 1)
    count = lax.axis_size("dp") * lax.axis_size("ctx")
    received = yield [
        lax.ppermute(
            lax.dynamic_index_in_dim(terms, place ^ mask, 0, keepdims=False),
            AXES,
            [(i, i ^ (mask << low)) for i in range(count)],
        )
        for mask in masks
    ]
    total = lax.dynamic_index_in_dim(terms, place, 0, keepdims=False).astype(f32)
    for value in received:
        total = total + value.astype(f32)
    return total.astype(terms.dtype)


class Process:
    def __init__(self, process):
        self.process = process
        self.arrived = next(process)
        self.result = None

    def advance(self):
        if self.result is not None:
            return
        try:
            self.arrived = self.process.send(self.arrived)
        except StopIteration as stop:
            self.arrived, self.result = [], stop.value

    def finish(self):
        while self.result is None:
            self.advance()
        return self.result


def together(processes, *others):
    flat = [value for process in processes for value in process.arrived]
    flat = list(lax.optimization_barrier(tuple(flat) + tuple(others)))
    for process in processes:
        count = len(process.arrived)
        process.arrived, flat = flat[:count], flat[count:]


def row_sum(values):
    return jnp.sum(values.astype(f32), axis=0)


def local(
    tokens,
    lengths,
    cotangent,
    query_proj,
    query_offset,
    key_proj,
    value_proj,
    value_offset,
    attn_proj,
    attn_offset,
    attn_gain,
    attn_shift,
    inner_proj,
    inner_offset,
    outer_proj,
    outer_offset,
    final_gain,
    final_shift,
):
    n_dp, n_ctx = lax.axis_size("dp"), lax.axis_size("ctx")
    n_dev = n_dp * n_ctx
    dev_bits = bits_of(n_dev)
    ctx_bits = bits_of(n_ctx)
    rows, width = tokens.shape
    seq = rows * n_ctx
    group = width // n_ctx
    part = width // n_dev
    hidden_width = inner_proj.shape[1]
    hidden_part = hidden_width // n_dev
    chunks = group // 128
    place = lax.axis_index("ctx")
    core_bit = ctx_bits
    up_bits = list(range(ctx_bits + 1, dev_bits))
    down_bits = up_bits[::-1]
    ctx_down = list(range(ctx_bits))[::-1]
    ctx_up = list(range(ctx_bits))

    vectors = jnp.concatenate(
        [
            query_offset,
            value_offset,
            attn_offset,
            attn_gain,
            attn_shift,
            outer_offset,
            final_gain,
            final_shift,
            inner_offset,
        ]
    ).astype(bf16)
    triple = jnp.stack([query_proj, key_proj, value_proj], axis=1).astype(bf16)
    by_group = triple.reshape(part, 3, n_ctx, group).transpose(2, 0, 1, 3)
    by_group = by_group.reshape(n_ctx, part, 3 * group)
    vector_rows = -(-vectors.shape[0] // (3 * group))
    vectors = jnp.pad(vectors, (0, vector_rows * 3 * group - vectors.shape[0]))
    vectors = vectors.reshape(vector_rows, 3 * group)
    vectors = jnp.pad(vectors, ((0, 16 - vector_rows), (0, 0)))
    packed = jnp.concatenate(
        [by_group, jnp.broadcast_to(vectors[None], (n_ctx,) + vectors.shape)], axis=1
    )

    first_shard = jnp.concatenate([attn_proj, inner_proj], axis=1).astype(bf16)
    w_first = lax.all_gather(first_shard, AXES, axis=0, tiled=True)
    w_outer = lax.all_gather(outer_proj.astype(bf16), AXES, axis=0, tiled=True)
    line = Process(gather_line(tokens))
    projections = Process(gather_group(packed, down_bits + [core_bit]))
    for turn in range(n_ctx - 1):
        together([line, projections])
        line.advance()
        projections.advance()
    tokens_all, packed = line.result, projections.finish()
    w_group = packed[:, :, :part].reshape(width, 3 * group)
    vectors = packed[:, :, part : part + vector_rows].reshape(n_dev, -1)
    names = [vectors[:, i * part : (i + 1) * part].reshape(width).astype(f32) for i in range(8)]
    b_query, b_value, b_attn, g_attn, s_attn, b_outer, g_final, s_final = names
    b_inner = vectors[:, 8 * part : 8 * part + hidden_part].reshape(1, hidden_width).astype(f32)

    b_group = lax.dynamic_slice_in_dim(
        jnp.stack([b_query, jnp.zeros_like(b_query), b_value]), place * group, group, 1
    ).reshape(3 * group)
    qkv = (jnp.dot(tokens_all, w_group, preferred_element_type=f32) + b_group).astype(bf16)
    where = jnp.stack(
        [place, lengths[0], own_bit(core_bit), lax.axis_index("dp") // 2]
    ).astype(jnp.int32)
    mixed_own, lse, mixed_parts = [], [], []
    for chunk in range(chunks):
        mixed_chunk, lse_chunk = attention_forward(qkv, where, rows, chunk, chunks)
        mixed_own.append(mixed_chunk)
        lse.append(lse_chunk)
        mixed_parts += exchange_slots(
            [mixed_chunk[slot * rows : (slot + 1) * rows] for slot in range(n_ctx)]
        )

    by_chunk = triple.reshape(part, 3, n_ctx, chunks, 128).transpose(0, 3, 2, 1, 4)
    by_chunk = by_chunk.reshape(part, 3 * width)
    by_chunk, _ = lax.optimization_barrier((by_chunk, qkv))
    w_triple = lax.all_gather(by_chunk, AXES, axis=0, tiled=True)
    none = jnp.zeros_like(b_attn)
    layer_vectors = jnp.stack([b_attn, g_attn, s_attn, b_outer, g_final, s_final, none, none])
    quads = n_dp // 2
    middle = layer_middle(
        where,
        tokens,
        cotangent,
        layer_vectors,
        b_inner,
        mixed_parts,
        n_ctx,
        (w_first, w_outer),
        quads,
    )
    layer_out, dfirst, sums, inner_sum = middle[:4]
    dmixed_slots = exchange_slots(middle[4 : 4 + n_ctx])

    gradients = middle[4 + n_ctx :]
    orders = (
        ctx_up[:1] + up_bits + ctx_up[1:],
        up_bits + ctx_up,
        down_bits + ctx_up,
    )
    sums_of, given = [], []
    for which, order in enumerate(orders):
        sent, kept = gradients[2 * which : 2 * which + 2]
        shard = sent.shape[0] * sent.shape[1] // 2 ** (dev_bits - 1)
        split = (2,) * (dev_bits - 1) + (shard, sent.shape[2])
        parts = [kept.reshape(split), swap(sent, core_bit).reshape(split)]
        sums_of.append(Process(scatter_sum(parts, order, f32, given)))
    dmixed_slots[0] = after(dmixed_slots[0], w_triple, *given)
    early = [sums[i].reshape(n_dev, part) for i in range(6)] + [inner_sum.reshape(n_dev, -1)]

    dqkv_rows, triples, late = [], [], []
    for chunk in range(chunks):
        dqkv = attention_backward(
            qkv, mixed_own[chunk], dmixed_slots, lse[chunk], where, chunk, chunks
        )
        if chunk == 0 and chunks > 1:
            together(sums_of[:2], dqkv)
            for one in sums_of[:2]:
                one.advance()
            dqkv_slots = [dqkv[slot * rows : (slot + 1) * rows] for slot in range(n_ctx)]
            dmixed_slots[0] = after(dmixed_slots[0], *given[3:], *dqkv_slots)
        dqkv_rows += exchange_slots(
            [dqkv[slot * rows : (slot + 1) * rows] for slot in range(n_ctx)]
        )
        grad_triple = lax.dot_general(
            tokens_all, dqkv, (((0,), (0,)), ((), ())), preferred_element_type=f32
        ).astype(bf16)
        triples.append(grad_triple.reshape((2,) * (dev_bits - ctx_bits) + (n_ctx, part, 384)))
        late.append(jnp.stack([row_sum(dqkv[:, :128]), row_sum(dqkv[:, 256:])]))
    triple_sum = jnp.concatenate(triples, axis=-1)
    together(sums_of, triple_sum, *dqkv_rows[:n_ctx])
    half_sum = triple_sum.reshape((quads, 2) + triple_sum.shape[dev_bits - ctx_bits :])
    half_sum = Process(scatter_core(half_sum, core_bit))
    for one in sums_of:
        one.advance()
    together(sums_of + [half_sum], *dqkv_rows[n_ctx:])
    half_sum.advance()
    triple_sum = Process(scatter_at_once(half_sum.result, up_bits))
    for one in sums_of:
        one.advance()
    together([one for one in sums_of if one.result is None] + [triple_sum])
    triple_sum.advance()
    triple_sum = Process(exchange_line(triple_sum.result))
    for one in sums_of:
        one.advance()
    triple_sum = triple_sum.finish()
    grad_triple = triple_sum.reshape(n_ctx, part, chunks, 3, 128).transpose(3, 1, 0, 2, 4)
    grad_triple = grad_triple.reshape(3, part, width).astype(f32)
    grad_left, grad_right, grad_outer = [one.finish() for one in sums_of]
    grad_attn = grad_left[:, :width]
    grad_inner = jnp.concatenate([grad_left[:, width:], grad_right], axis=1)
    late = jnp.concatenate(late, axis=1)
    late = lax.dynamic_update_slice_in_dim(
        jnp.zeros((2, width), f32), late, place * group, 1
    )
    late = late.reshape(2, n_dev, part).transpose(1, 0, 2).reshape(n_dev, 2 * part)
    early = jnp.concatenate(early + [late], axis=1)
    early = lax.all_to_all(early, AXES, 0, 0, tiled=True).sum(axis=0)
    late = early[early.shape[0] - 2 * part :].reshape(2, part)
    input_grad = input_gradient(where, dfirst, w_triple, dqkv_rows, n_ctx)

    pieces = [early[i * part : (i + 1) * part] for i in range(6)]
    return (
        layer_out,
        input_grad,
        grad_triple[0],
        late[0],
        grad_triple[1],
        grad_triple[2],
        late[1],
        grad_attn,
        pieces[3],
        pieces[4],
        pieces[5],
        grad_inner,
        early[6 * part : 6 * part + hidden_part],
        grad_outer,
        pieces[0],
        pieces[1],
        pieces[2],
    )


def solution(mesh):
    rows, vector = P(AXES, None), P(AXES)
    in_specs = (rows, P("dp"), rows, rows, vector, rows, rows, vector, rows) + (vector,) * 3
    in_specs += (rows, vector, rows) + (vector,) * 3
    out_specs = (rows,) * 3 + (vector, rows, rows, vector, rows) + (vector,) * 3
    out_specs += (rows, vector, rows) + (vector,) * 3
    return jax.shard_map(local, mesh=mesh, in_specs=in_specs, out_specs=out_specs, check_vma=False)
```

```python
import functools
import math

import jax
import jax.numpy as jnp
from jax import lax
from jax.experimental import pallas as pl
from jax.experimental.pallas import tpu as pltpu
from jax.sharding import PartitionSpec as P

HD = 64
AXES = ("dp", "ctx")
norm_eps = 1e-05
score_scale = 1.0 / math.sqrt(HD)
score_scale_two = score_scale * math.log2(math.e)
f32 = jnp.float32
bf16 = jnp.bfloat16


def kernel_cost(flops):
    return flops // 8


def attention_forward_kernel(
    place_ref, q_ref, k_ref, v_ref, mixed_ref, lse_ref, keys_t_ref, *, heads, rows
):
    width = k_ref.shape[1]
    seq = keys_t_ref.shape[1]

    @pl.when(pl.program_id(0) == 0)
    def _():
        keys_t_ref[...] = k_ref[...].T

    queries = q_ref[...]
    keys_t = keys_t_ref[...]
    values = v_ref[...]
    slots = [
        (place_ref[0] ^ slot) * rows + lax.broadcasted_iota(jnp.int32, (1, rows), 1)
        for slot in range(seq // rows)
    ]
    key_pos = jnp.concatenate(slots, axis=1)
    bias = jnp.where(key_pos < place_ref[1], 0.0, -1e30).astype(f32)
    head_of = lax.broadcasted_iota(jnp.int32, (rows, width), 1) // HD
    lane = lax.broadcasted_iota(jnp.int32, (rows, 128), 1)
    mixed = jnp.zeros((rows, width), f32)
    lse = jnp.zeros((rows, 128), f32)
    for head in range(heads):
        own = jnp.where(head_of == head, queries, jnp.zeros_like(queries))
        scores = jnp.dot(own, keys_t, preferred_element_type=f32) * score_scale_two + bias
        top = jnp.max(scores, axis=1, keepdims=True)
        probs = jnp.exp2(scores - top)
        total = jnp.sum(probs, axis=1, keepdims=True)
        part = jnp.dot(probs.astype(bf16), values, preferred_element_type=f32)
        mixed = jnp.where(head_of == head, part * (1.0 / total), mixed)
        lse = jnp.where(lane == head, top + jnp.log2(total), lse)
    mixed_ref[...] = mixed.astype(bf16)
    lse_ref[...] = lse.T[:8]


def attention_forward(qkv, place, rows, chunk, chunks):
    seq = qkv.shape[0]
    width = qkv.shape[1] // (3 * chunks)
    heads = width // HD
    return pl.pallas_call(
        functools.partial(attention_forward_kernel, heads=heads, rows=rows),
        grid=(seq // rows,),
        in_specs=[
            pl.BlockSpec(memory_space=pltpu.SMEM),
            pl.BlockSpec((rows, width), lambda i: (i, chunk)),
            pl.BlockSpec((seq, width), lambda i: (0, chunks + chunk)),
            pl.BlockSpec((seq, width), lambda i: (0, 2 * chunks + chunk)),
        ],
        out_specs=[
            pl.BlockSpec((rows, width), lambda i: (i, 0)),
            pl.BlockSpec((8, rows), lambda i: (0, i)),
        ],
        out_shape=[
            jax.ShapeDtypeStruct((seq, width), bf16),
            jax.ShapeDtypeStruct((8, seq), f32),
        ],
        scratch_shapes=[pltpu.VMEM((width, seq), bf16)],
        compiler_params=pltpu.CompilerParams(vmem_limit_bytes=56 * 2**20),
        cost_estimate=pl.CostEstimate(
            flops=kernel_cost(16 * seq * seq * width),
            bytes_accessed=8 * seq * width,
            transcendentals=seq * seq * heads,
        ),
        name="attention_forward",
    )(place, qkv, qkv, qkv)


def attention_backward_kernel(
    place_ref,
    q_ref,
    k_ref,
    v_ref,
    mixed_ref,
    lse_ref,
    *refs,
    heads,
    rows,
):
    step = pl.program_id(0)
    dmixed_refs, (out_ref, placed_ref, keys_t_ref, dk_sum, dv_sum, dmixed_ref) = refs[:-6], refs[-6:]
    seq, width = dk_sum.shape
    for slot, slot_ref in enumerate(dmixed_refs):

        @pl.when(step == slot)
        def _(slot_ref=slot_ref):
            dmixed_ref[...] = slot_ref[...]

    @pl.when(step == 0)
    def _():
        keys_t_ref[...] = k_ref[...].T
        dk_sum[...] = jnp.zeros_like(dk_sum)
        dv_sum[...] = jnp.zeros_like(dv_sum)

    queries, dmixed = q_ref[...], dmixed_ref[...]
    queries_t, dmixed_t, mixed_t = queries.T, dmixed.T, mixed_ref[...].T
    product = dmixed_t.astype(f32) * mixed_t.astype(f32)
    lane_head = lax.broadcasted_iota(jnp.int32, (rows, width), 1) // HD
    row_head = lax.broadcasted_iota(jnp.int32, (width, rows), 0) // HD
    none, none_t = jnp.zeros_like(queries), jnp.zeros_like(queries_t)
    lse = lse_ref[...]
    per_head = []
    for head in range(heads):
        per_head.append(
            (
                jnp.where(row_head == head, queries_t, none_t),
                jnp.where(row_head == head, dmixed_t, none_t),
                jnp.where(lane_head == head, queries, none),
                jnp.where(lane_head == head, dmixed, none),
                jnp.sum(product[HD * head : HD * head + HD], axis=0, keepdims=True),
                lse[head : head + 1],
            )
        )

    def chunk(index, dq_t):
        span = pl.ds(pl.multiple_of(index * rows, rows), rows)
        keys, values = k_ref[span, :], v_ref[span, :]
        key_pos = (place_ref[0] ^ index) * rows + lax.broadcasted_iota(jnp.int32, (rows, 1), 0)
        bias = jnp.where(key_pos < place_ref[1], 0.0, -1e30).astype(f32)
        dk, dv = dk_sum[span, :], dv_sum[span, :]
        new_dq_t = []
        for head in range(heads):
            own_q_t, own_do_t, own_q, own_do, delta, own_lse = per_head[head]
            scores = jnp.dot(keys, own_q_t, preferred_element_type=f32)
            probs = jnp.exp2(scores * score_scale_two + bias - own_lse)
            dprobs = jnp.dot(values, own_do_t, preferred_element_type=f32)
            dscores = (probs * (dprobs - delta)).astype(bf16)
            dv = dv + jnp.dot(probs.astype(bf16), own_do, preferred_element_type=f32)
            dk = dk + jnp.dot(dscores, own_q, preferred_element_type=f32)
            own_keys_t = keys_t_ref[HD * head : HD * head + HD, span]
            new_dq_t.append(
                dq_t[head] + jnp.dot(own_keys_t, dscores, preferred_element_type=f32)
            )
        dk_sum[span, :] = dk
        dv_sum[span, :] = dv
        return tuple(new_dq_t)

    start = tuple(jnp.zeros((HD, rows), f32) for _ in range(heads))
    dq_t = jnp.concatenate(lax.fori_loop(0, seq // rows, chunk, start), axis=0)
    own_rows = pl.ds(pl.multiple_of(step * rows, rows), rows)
    out_ref[own_rows, :width] = (dq_t * score_scale).T.astype(bf16)

    @pl.when(step == pl.num_programs(0) - 1)
    def _():
        out_ref[:, width : 2 * width] = (dk_sum[...] * score_scale).astype(bf16)
        out_ref[:, 2 * width :] = dv_sum[...].astype(bf16)
        for slot in range(seq // rows):
            placed_ref[place_ref[0] ^ slot] = out_ref[slot * rows : (slot + 1) * rows, :]


def attention_backward(qkv, mixed, dmixed_slots, lse, place, chunk, chunks):
    seq, width = mixed.shape
    rows = seq // len(dmixed_slots)
    heads = width // HD
    block = pl.BlockSpec((rows, width), lambda i: (i, 0))
    return pl.pallas_call(
        functools.partial(attention_backward_kernel, heads=heads, rows=rows),
        grid=(seq // rows,),
        in_specs=[
            pl.BlockSpec(memory_space=pltpu.SMEM),
            pl.BlockSpec((rows, width), lambda i: (i, chunk)),
            pl.BlockSpec((seq, width), lambda i: (0, chunks + chunk)),
            pl.BlockSpec((seq, width), lambda i: (0, 2 * chunks + chunk)),
            block,
            pl.BlockSpec((8, rows), lambda i: (0, i)),
        ]
        + [pl.BlockSpec((rows, width), lambda i: (0, chunk))] * len(dmixed_slots),
        out_specs=[
            pl.BlockSpec((seq, 3 * width), lambda i: (0, 0)),
            pl.BlockSpec((seq // rows, rows, 3 * width), lambda i: (0, 0, 0)),
        ],
        out_shape=[
            jax.ShapeDtypeStruct((seq, 3 * width), bf16),
            jax.ShapeDtypeStruct((seq // rows, rows, 3 * width), bf16),
        ],
        scratch_shapes=[
            pltpu.VMEM((width, seq), bf16),
            pltpu.VMEM((seq, width), f32),
            pltpu.VMEM((seq, width), f32),
            pltpu.VMEM((rows, width), bf16),
        ],
        compiler_params=pltpu.CompilerParams(vmem_limit_bytes=56 * 2**20),
        cost_estimate=pl.CostEstimate(
            flops=kernel_cost(40 * seq * seq * width),
            bytes_accessed=16 * seq * width,
            transcendentals=seq * seq * heads,
        ),
        name="attention_backward",
    )(place, qkv, qkv, qkv, mixed, lse, *dmixed_slots)


def layer_kernel(
    place_ref,
    tokens_ref,
    cotangent_ref,
    vectors_ref,
    inner_offset_ref,
    *refs,
    chunks,
    groups,
):
    mixed_refs, refs = refs[: chunks * groups], refs[chunks * groups :]
    weight_refs, refs = refs[:2], refs[2:]
    (layer_out_ref, dfirst_ref, sums_ref, inner_sum_ref), refs = refs[:4], refs[4:]
    dmixed_refs, gradient_refs, refs = refs[:groups], refs[groups : groups + 4], refs[groups + 4 :]
    (w_attn, w_inner, w_outer), refs = refs[:3], refs[3:]
    (mixed_ref, hidden_ref, act_ref, douter_ref, dpre_ref, dattn_ref), refs = refs[:6], refs[6:]
    (wide_ref, normed_ref, inverse_ref, total_ref, dmixed_ref, turned_ref, sems) = refs
    rows, width = tokens_ref.shape
    hidden_width = w_inner.shape[1]
    place, length, core, quad = place_ref[0], place_ref[1], place_ref[2], place_ref[3]
    first_row = place * rows

    first_weights, outer_weights = weight_refs
    copies = [
        pltpu.make_async_copy(first_weights.at[:, :width], w_attn, sems.at[0]),
        pltpu.make_async_copy(first_weights.at[:, width:], w_inner, sems.at[1]),
        pltpu.make_async_copy(outer_weights, w_outer, sems.at[2]),
    ]
    for copy in copies:
        copy.start()

    b_attn, g_attn, s_attn = vectors_ref[0:1], vectors_ref[1:2], vectors_ref[2:3]
    b_outer, g_final, s_final = vectors_ref[3:4], vectors_ref[4:5], vectors_ref[5:6]
    chunk_width = mixed_refs[0].shape[1]

    def columns_of(chunk, slot):
        start = ((place ^ slot) * chunks + chunk) * chunk_width
        return pl.ds(pl.multiple_of(start, chunk_width), chunk_width)

    for chunk in range(chunks):
        for slot in range(groups):
            mixed_ref[:, columns_of(chunk, slot)] = mixed_refs[chunk * groups + slot][...]

    copies[0].wait()

    step = 128

    def norm_one(turn, carried):
        span = pl.ds(pl.multiple_of(turn * step, step), step)
        first = (
            tokens_ref[span, :].astype(f32)
            + jnp.dot(mixed_ref[span, :], w_attn[...], preferred_element_type=f32)
            + b_attn
        )
        centered = first - jnp.mean(first, axis=1, keepdims=True)
        inverse = lax.rsqrt(jnp.mean(centered * centered, axis=1, keepdims=True) + norm_eps)
        normed = centered * inverse
        hidden = normed * g_attn + s_attn
        normed_ref[span, :] = normed
        inverse_ref[span, :] = jnp.broadcast_to(inverse, (step, 128))
        total_ref[span, :] = hidden
        hidden_ref[span, :] = hidden.astype(bf16)
        return carried

    lax.fori_loop(0, rows // step, norm_one, 0)

    copies[1].wait()
    block = 512

    def feed_in(turn, carried):
        span = pl.ds(pl.multiple_of(turn * block, block), block)
        pre = (
            jnp.dot(hidden_ref[...], w_inner[:, span], preferred_element_type=f32)
            + inner_offset_ref[:, span]
        )
        normal_cdf = 0.5 * (1.0 + lax.erf(pre * (1.0 / math.sqrt(2.0))))
        act_ref[:, span] = (pre * normal_cdf).astype(bf16)
        slope = normal_cdf + pre * jnp.exp(-0.5 * pre * pre) * (1.0 / math.sqrt(2.0 * math.pi))
        dpre_ref[:, span] = slope.astype(bf16)
        return carried

    lax.fori_loop(0, hidden_width // block, feed_in, 0)

    copies[2].wait()
    narrow = 512

    def feed_out(turn, carried):
        span = pl.ds(pl.multiple_of(turn * narrow, narrow), narrow)
        wide_ref[:, span] = jnp.dot(act_ref[...], w_outer[:, span], preferred_element_type=f32)
        return carried

    lax.fori_loop(0, width // narrow, feed_out, 0)

    def norm_two(turn, carried):
        span = pl.ds(pl.multiple_of(turn * step, step), step)
        second = total_ref[span, :] + wide_ref[span, :] + b_outer
        centered = second - jnp.mean(second, axis=1, keepdims=True)
        inverse = lax.rsqrt(jnp.mean(centered * centered, axis=1, keepdims=True) + norm_eps)
        normed = centered * inverse
        row = first_row + turn * step + lax.broadcasted_iota(jnp.int32, (step, 1), 0)
        valid = jnp.where(row < length, 1.0, 0.0).astype(f32)
        layer_out_ref[span, :] = ((normed * g_final + s_final) * valid).astype(bf16)
        upstream = cotangent_ref[span, :].astype(f32) * valid
        shift_sum, gain_sum, offset_sum = carried
        shift_sum = shift_sum + jnp.sum(upstream, axis=0, keepdims=True)
        gain_sum = gain_sum + jnp.sum(upstream * normed, axis=0, keepdims=True)
        scaled = upstream * g_final
        first_mean = jnp.mean(scaled, axis=1, keepdims=True)
        second_mean = jnp.mean(scaled * normed, axis=1, keepdims=True)
        dsecond = inverse * (scaled - first_mean - normed * second_mean)
        total_ref[span, :] = dsecond
        douter = dsecond.astype(bf16)
        douter_ref[span, :] = douter
        offset_sum = offset_sum + jnp.sum(douter.astype(f32), axis=0, keepdims=True)
        return (shift_sum, gain_sum, offset_sum)

    none = jnp.zeros((1, width), f32)
    shift_sum, gain_sum, offset_sum = lax.fori_loop(
        0, rows // step, norm_two, (none, none, none)
    )
    sums_ref[0:1] = offset_sum
    sums_ref[1:2] = gain_sum
    sums_ref[2:3] = shift_sum

    across = (((1,), (1,)), ((), ()))

    def back_out(turn, carried):
        span = pl.ds(pl.multiple_of(turn * block, block), block)
        dact = lax.dot_general(
            douter_ref[...], w_outer[span, :], across, preferred_element_type=f32
        )
        dpre = (dact * dpre_ref[:, span].astype(f32)).astype(bf16)
        dpre_ref[:, span] = dpre
        inner_sum_ref[:, span] = jnp.sum(dpre.astype(f32), axis=0, keepdims=True)
        return carried

    lax.fori_loop(0, hidden_width // block, back_out, 0)

    quads = gradient_refs[0].shape[0]
    slab, outer_slab = width // (2 * quads), hidden_width // (2 * quads)
    down = (((0,), (0,)), ((), ()))

    def leave(first_sem, source, which, to_col, height):
        started = []
        levels = quads.bit_length() - 1
        if which == 0:
            order = [
                sum(((slot >> i) & 1) << (levels - 1 - i) for i in range(levels))
                for slot in range(quads)
            ]
        else:
            order = list(range(quads))
        for side in range(2):
            owner = 1 - core if side == 0 else core
            for slot in range(quads):
                row = pl.multiple_of((2 * (order[slot] ^ quad) + owner) * height, height)
                copy = pltpu.make_async_copy(
                    source.at[pl.ds(row, height), :],
                    gradient_refs[2 * which + side].at[slot, :, to_col : to_col + source.shape[1]],
                    sems.at[first_sem + len(started)],
                )
                copy.start()
                started.append(copy)
        return started

    def outer_gradient(turn, carried):
        span = pl.ds(pl.multiple_of(turn * block, block), block)
        terms = lax.dot_general(
            act_ref[:, span], douter_ref[...], down, preferred_element_type=f32
        )
        w_outer[span, :] = terms.astype(bf16)
        return carried

    lax.fori_loop(0, hidden_width // block, outer_gradient, 0)
    leaving = leave(3, w_outer, 1, 0, outer_slab)

    def back_in(turn, carried):
        span = pl.ds(pl.multiple_of(turn * narrow, narrow), narrow)
        wide_ref[:, span] = lax.dot_general(
            dpre_ref[...], w_inner[span, :], across, preferred_element_type=f32
        )
        return carried

    lax.fori_loop(0, width // narrow, back_in, 0)

    def norm_one_back(turn, carried):
        span = pl.ds(pl.multiple_of(turn * step, step), step)
        dhidden = total_ref[span, :] + wide_ref[span, :]
        normed = normed_ref[span, :]
        inverse = inverse_ref[span, 0:1]
        shift_sum, gain_sum, offset_sum = carried
        shift_sum = shift_sum + jnp.sum(dhidden, axis=0, keepdims=True)
        gain_sum = gain_sum + jnp.sum(dhidden * normed, axis=0, keepdims=True)
        scaled = dhidden * g_attn
        first_mean = jnp.mean(scaled, axis=1, keepdims=True)
        second_mean = jnp.mean(scaled * normed, axis=1, keepdims=True)
        dfirst = inverse * (scaled - first_mean - normed * second_mean)
        dfirst_ref[span, :] = dfirst
        dattn = dfirst.astype(bf16)
        dattn_ref[span, :] = dattn
        offset_sum = offset_sum + jnp.sum(dattn.astype(f32), axis=0, keepdims=True)
        dmixed = lax.dot_general(dattn, w_attn[...], across, preferred_element_type=f32)
        dmixed_ref[span, :] = dmixed.astype(bf16)
        return (shift_sum, gain_sum, offset_sum)

    shift_sum, gain_sum, offset_sum = lax.fori_loop(
        0, rows // step, norm_one_back, (none, none, none)
    )
    sums_ref[3:4] = offset_sum
    sums_ref[4:5] = gain_sum
    sums_ref[5:6] = shift_sum
    sums_ref[6:8] = jnp.zeros((2, width), f32)
    group_width = chunks * chunk_width
    for slot in range(groups):
        start = pl.multiple_of((place ^ slot) * group_width, group_width)
        dmixed_refs[slot][...] = dmixed_ref[:, pl.ds(start, group_width)]

    turned_ref[...] = hidden_ref[...].T
    wide_block = 1024

    def inner_gradient(turn, carried):
        span = pl.ds(pl.multiple_of(turn * wide_block, wide_block), wide_block)
        for half in range(width // block):
            rows_of = slice(half * block, (half + 1) * block)
            terms = jnp.dot(turned_ref[rows_of, :], dpre_ref[:, span], preferred_element_type=f32)
            w_inner[rows_of, span] = terms.astype(bf16)
        return carried

    lax.fori_loop(0, hidden_width // wide_block, inner_gradient, 0)
    leaving += leave(3 + len(leaving), w_inner, 0, width, slab)
    turned_ref[...] = mixed_ref[...].T
    for half in range(width // block):
        rows_of = slice(half * block, (half + 1) * block)
        terms = jnp.dot(turned_ref[rows_of, :], dattn_ref[...], preferred_element_type=f32)
        w_attn[rows_of, :] = terms.astype(bf16)
    leaving += leave(3 + len(leaving), w_attn, 0, 0, slab)
    for copy in leaving:
        copy.wait()


def layer_middle(place, tokens, cotangent, vectors, inner_offset, mixed_parts, groups, weights, quads):
    rows, width = tokens.shape
    hidden_width = inner_offset.shape[1]
    chunk_width = mixed_parts[0].shape[1]
    chunks = len(mixed_parts) // groups
    slab, outer_slab = width // (2 * quads), hidden_width // (2 * quads)
    vmem = pl.BlockSpec(memory_space=pltpu.VMEM)
    anywhere = pl.BlockSpec(memory_space=pl.ANY)
    shapes = [
        jax.ShapeDtypeStruct((rows, width), bf16),
        jax.ShapeDtypeStruct((rows, width), f32),
        jax.ShapeDtypeStruct((8, width), f32),
        jax.ShapeDtypeStruct((1, hidden_width), f32),
    ] + [jax.ShapeDtypeStruct((rows, chunks * chunk_width), bf16)] * groups
    gradients = [
        jax.ShapeDtypeStruct((quads, slab, width + hidden_width), bf16),
        jax.ShapeDtypeStruct((quads, outer_slab, width), bf16),
    ]
    gradients = [shape for shape in gradients for _ in range(2)]
    return pl.pallas_call(
        functools.partial(layer_kernel, chunks=chunks, groups=groups),
        in_specs=[pl.BlockSpec(memory_space=pltpu.SMEM)]
        + [vmem] * (4 + chunks * groups)
        + [anywhere] * 2,
        out_specs=[vmem] * len(shapes) + [anywhere] * 4,
        out_shape=shapes + gradients,
        scratch_shapes=[
            pltpu.VMEM((width, width), bf16),
            pltpu.VMEM((width, hidden_width), bf16),
            pltpu.VMEM((hidden_width, width), bf16),
            pltpu.VMEM((rows, width), bf16),
            pltpu.VMEM((rows, width), bf16),
            pltpu.VMEM((rows, hidden_width), bf16),
            pltpu.VMEM((rows, width), bf16),
            pltpu.VMEM((rows, hidden_width), bf16),
            pltpu.VMEM((rows, width), bf16),
            pltpu.VMEM((rows, width), f32),
            pltpu.VMEM((rows, width), f32),
            pltpu.VMEM((rows, 128), f32),
            pltpu.VMEM((rows, width), f32),
            pltpu.VMEM((rows, width), bf16),
            pltpu.VMEM((width, rows), bf16),
            pltpu.SemaphoreType.DMA((3 + 6 * quads,)),
        ],
        compiler_params=pltpu.CompilerParams(vmem_limit_bytes=60 * 2**20),
        cost_estimate=pl.CostEstimate(
            flops=kernel_cost(12 * rows * width * (hidden_width + width)),
            bytes_accessed=4 * width * (2 * hidden_width + width) + 10 * rows * width,
            transcendentals=2 * rows * hidden_width,
        ),
        name="layer_middle",
    )(place, tokens, cotangent, vectors, inner_offset, *mixed_parts, *weights)


def input_kernel(place_ref, dfirst_ref, weights_ref, *refs, slotted, placed, groups):
    slots, parts, (out_ref, rows_ref) = refs[:slotted], refs[slotted:-2], refs[-2:]
    cols = weights_ref.shape[1] // (groups * (slotted // groups + placed))
    chunk = 0
    for first in range(0, slotted, groups):
        for slot in range(groups):
            start = (chunk * groups + (place_ref[0] ^ slot)) * cols
            span = pl.ds(pl.multiple_of(start, cols), cols)
            rows_ref[:, span] = slots[first + slot][...]
        chunk += 1
    for part in parts:
        for group in range(groups):
            start = (chunk * groups + group) * cols
            rows_ref[:, start : start + cols] = part[group]
        chunk += 1
    block = 512

    def columns(turn, carried):
        span = pl.ds(pl.multiple_of(turn * block, block), block)
        terms = lax.dot_general(
            rows_ref[...],
            weights_ref[span, :],
            (((1,), (1,)), ((), ())),
            preferred_element_type=f32,
        )
        out_ref[:, span] = (dfirst_ref[:, span] + terms).astype(bf16)
        return carried

    lax.fori_loop(0, out_ref.shape[1] // block, columns, 0)


def input_gradient(place, dfirst, weights, slots, parts, groups):
    rows, width = dfirst.shape
    vmem = pl.BlockSpec(memory_space=pltpu.VMEM)
    given = list(slots) + list(parts)
    return pl.pallas_call(
        functools.partial(input_kernel, slotted=len(slots), placed=len(parts), groups=groups),
        in_specs=[pl.BlockSpec(memory_space=pltpu.SMEM)] + [vmem] * (2 + len(given)),
        out_specs=vmem,
        out_shape=jax.ShapeDtypeStruct((rows, width), bf16),
        scratch_shapes=[pltpu.VMEM((rows, weights.shape[1]), bf16)],
        compiler_params=pltpu.CompilerParams(vmem_limit_bytes=48 * 2**20),
        cost_estimate=pl.CostEstimate(
            flops=kernel_cost(2 * rows * width * weights.shape[1]),
            bytes_accessed=2 * width * weights.shape[1] + 12 * rows * width,
            transcendentals=0,
        ),
        name="input_gradient",
    )(place, dfirst, weights, *given)


def device_index():
    return lax.axis_index("dp") * lax.axis_size("ctx") + lax.axis_index("ctx")


def bits_of(count):
    return count.bit_length() - 1


def swap(values, bit):
    count = lax.axis_size("dp") * lax.axis_size("ctx")
    return lax.ppermute(values, AXES, [(i, i ^ (1 << bit)) for i in range(count)])


def own_bit(bit):
    return (device_index() >> bit) & 1


def joined(shard, other, bit, axis):
    return jnp.where(
        own_bit(bit) == 1,
        jnp.stack([other, shard], axis=axis),
        jnp.stack([shard, other], axis=axis),
    )


def after(value, *others):
    return lax.optimization_barrier((value,) + others)[0]


def gather_line(block):
    count = lax.axis_size("ctx")
    place = lax.axis_index("ctx")
    held = jnp.broadcast_to(block[None], (count,) + block.shape)
    from_left = from_right = block
    for step in range(1, count):
        from_left, from_right = yield [
            lax.ppermute(from_left, "ctx", [(i, i + 1) for i in range(count - 1)]),
            lax.ppermute(from_right, "ctx", [(i + 1, i) for i in range(count - 1)]),
        ]
        for arrived, source in ((from_left, place - step), (from_right, place + step)):
            inside = (source >= 0) & (source < count)
            held = lax.dynamic_update_index_in_dim(
                held,
                jnp.where(inside, arrived, block),
                jnp.where(inside, source ^ place, 0),
                0,
            )
    return held.reshape((count * block.shape[0],) + block.shape[1:])


def exchange_slots(slots):
    count = lax.axis_size("ctx")
    return [slots[0]] + [
        lax.ppermute(slots[mask], "ctx", [(i, i ^ mask) for i in range(count)])
        for mask in range(1, count)
    ]


def exchange_line(blocks):
    count = lax.axis_size("ctx")
    place = lax.axis_index("ctx")
    arrived = yield [
        lax.ppermute(
            lax.dynamic_index_in_dim(blocks, place ^ mask, 0, keepdims=False),
            "ctx",
            [(i, i ^ mask) for i in range(count)],
        )
        for mask in range(1, count)
    ]
    for mask, value in enumerate(arrived, 1):
        blocks = lax.dynamic_update_index_in_dim(blocks, value, place ^ mask, 0)
    return blocks


def gather_bits(shard, bit_order):
    held = []
    for bit in bit_order:
        (other,) = yield [swap(shard, bit)]
        held = sorted(held + [bit], reverse=True)
        shard = joined(shard, other, bit, held.index(bit))
    return shard.reshape((2 ** len(held),) + shard.shape[len(held) :])


def gather_group(packed, bit_order):
    packed = yield from exchange_line(packed)
    return (yield from gather_bits(packed, bit_order))


def scatter_sum(parts, bit_order, out_dtype, sent):
    left = sorted([bit for bit in bit_order if bit < bits_of(lax.axis_size("ctx"))], reverse=True)
    for bit in bit_order:
        if bit not in left:
            given, parts = [part[1] for part in parts], [part[0] for part in parts]
        else:
            axis, mine = left.index(bit), own_bit(bit)
            given = [lax.dynamic_index_in_dim(part, 1 - mine, axis, False) for part in parts]
            parts = [lax.dynamic_index_in_dim(part, mine, axis, False) for part in parts]
        given = total_of(given, parts[0].dtype)
        sent.append(given)
        kept = total_of(parts, parts[0].dtype)
        parts = [kept] + (yield [swap(given, bit)])
        if bit in left:
            left.remove(bit)
    return total_of(parts, out_dtype)


def total_of(parts, dtype):
    total = parts[0].astype(f32)
    for part in parts[1:]:
        total = total + part.astype(f32)
    return total.astype(dtype)


def scatter_core(terms, bit):
    mine = own_bit(bit)
    (received,) = yield [swap(lax.dynamic_index_in_dim(terms, 1 - mine, 1, False), bit)]
    kept = lax.dynamic_index_in_dim(terms, mine, 1, False)
    return total_of([kept, received], terms.dtype)


def scatter_at_once(terms, bits):
    masks = range(1, 2 ** len(bits))
    low = min(bits)
    place = (device_index() >> low) & (2 ** len(bits) - 1)
    count = lax.axis_size("dp") * lax.axis_size("ctx")
    received = yield [
        lax.ppermute(
            lax.dynamic_index_in_dim(terms, place ^ mask, 0, keepdims=False),
            AXES,
            [(i, i ^ (mask << low)) for i in range(count)],
        )
        for mask in masks
    ]
    total = lax.dynamic_index_in_dim(terms, place, 0, keepdims=False).astype(f32)
    for value in received:
        total = total + value.astype(f32)
    return total.astype(terms.dtype)


class Process:
    def __init__(self, process):
        self.process = process
        self.arrived = next(process)
        self.result = None

    def advance(self):
        if self.result is not None:
            return
        try:
            self.arrived = self.process.send(self.arrived)
        except StopIteration as stop:
            self.arrived, self.result = [], stop.value

    def finish(self):
        while self.result is None:
            self.advance()
        return self.result


def together(processes, *others):
    flat = [value for process in processes for value in process.arrived]
    flat = list(lax.optimization_barrier(tuple(flat) + tuple(others)))
    for process in processes:
        count = len(process.arrived)
        process.arrived, flat = flat[:count], flat[count:]


def row_sum(values):
    return jnp.sum(values.astype(f32), axis=0)


def local(
    tokens,
    lengths,
    cotangent,
    query_proj,
    query_offset,
    key_proj,
    value_proj,
    value_offset,
    attn_proj,
    attn_offset,
    attn_gain,
    attn_shift,
    inner_proj,
    inner_offset,
    outer_proj,
    outer_offset,
    final_gain,
    final_shift,
):
    n_dp, n_ctx = lax.axis_size("dp"), lax.axis_size("ctx")
    n_dev = n_dp * n_ctx
    dev_bits = bits_of(n_dev)
    ctx_bits = bits_of(n_ctx)
    rows, width = tokens.shape
    seq = rows * n_ctx
    group = width // n_ctx
    part = width // n_dev
    hidden_width = inner_proj.shape[1]
    hidden_part = hidden_width // n_dev
    chunks = group // 128
    place = lax.axis_index("ctx")
    core_bit = ctx_bits
    up_bits = list(range(ctx_bits + 1, dev_bits))
    down_bits = up_bits[::-1]
    ctx_down = list(range(ctx_bits))[::-1]
    ctx_up = list(range(ctx_bits))

    vectors = jnp.concatenate(
        [
            query_offset,
            value_offset,
            attn_offset,
            attn_gain,
            attn_shift,
            outer_offset,
            final_gain,
            final_shift,
            inner_offset,
        ]
    ).astype(bf16)
    triple = jnp.stack([query_proj, key_proj, value_proj], axis=1).astype(bf16)
    by_group = triple.reshape(part, 3, n_ctx, group).transpose(2, 0, 1, 3)
    by_group = by_group.reshape(n_ctx, part, 3 * group)
    vector_rows = -(-vectors.shape[0] // (3 * group))
    vectors = jnp.pad(vectors, (0, vector_rows * 3 * group - vectors.shape[0]))
    vectors = vectors.reshape(vector_rows, 3 * group)
    vectors = jnp.pad(vectors, ((0, 16 - vector_rows), (0, 0)))
    packed = jnp.concatenate(
        [by_group, jnp.broadcast_to(vectors[None], (n_ctx,) + vectors.shape)], axis=1
    )

    first_shard = jnp.concatenate([attn_proj, inner_proj], axis=1).astype(bf16)
    w_first = lax.all_gather(first_shard, AXES, axis=0, tiled=True)
    w_outer = lax.all_gather(outer_proj.astype(bf16), AXES, axis=0, tiled=True)
    line = Process(gather_line(tokens))
    projections = Process(gather_group(packed, down_bits + [core_bit]))
    for turn in range(n_ctx - 1):
        together([line, projections])
        line.advance()
        projections.advance()
    tokens_all, packed = line.result, projections.finish()
    w_group = packed[:, :, :part].reshape(width, 3 * group)
    vectors = packed[:, :, part : part + vector_rows].reshape(n_dev, -1)
    names = [vectors[:, i * part : (i + 1) * part].reshape(width).astype(f32) for i in range(8)]
    b_query, b_value, b_attn, g_attn, s_attn, b_outer, g_final, s_final = names
    b_inner = vectors[:, 8 * part : 8 * part + hidden_part].reshape(1, hidden_width).astype(f32)

    b_group = lax.dynamic_slice_in_dim(
        jnp.stack([b_query, jnp.zeros_like(b_query), b_value]), place * group, group, 1
    ).reshape(3 * group)
    qkv = (jnp.dot(tokens_all, w_group, preferred_element_type=f32) + b_group).astype(bf16)
    where = jnp.stack(
        [place, lengths[0], own_bit(core_bit), lax.axis_index("dp") // 2]
    ).astype(jnp.int32)
    mixed_own, lse, mixed_parts = [], [], []
    for chunk in range(chunks):
        mixed_chunk, lse_chunk = attention_forward(qkv, where, rows, chunk, chunks)
        mixed_own.append(mixed_chunk)
        lse.append(lse_chunk)
        mixed_parts += exchange_slots(
            [mixed_chunk[slot * rows : (slot + 1) * rows] for slot in range(n_ctx)]
        )

    by_chunk = triple.reshape(part, 3, n_ctx, chunks, 128).transpose(0, 3, 2, 1, 4)
    by_chunk = by_chunk.reshape(part, 3 * width)
    by_chunk, _ = lax.optimization_barrier((by_chunk, qkv))
    w_triple = lax.all_gather(by_chunk, AXES, axis=0, tiled=True)
    none = jnp.zeros_like(b_attn)
    layer_vectors = jnp.stack([b_attn, g_attn, s_attn, b_outer, g_final, s_final, none, none])
    quads = n_dp // 2
    middle = layer_middle(
        where,
        tokens,
        cotangent,
        layer_vectors,
        b_inner,
        mixed_parts,
        n_ctx,
        (w_first, w_outer),
        quads,
    )
    layer_out, dfirst, sums, inner_sum = middle[:4]
    dmixed_slots = exchange_slots(middle[4 : 4 + n_ctx])

    gradients = middle[4 + n_ctx :]
    orders = (
        up_bits + ctx_up,
        down_bits + ctx_down,
    )
    sums_of, given = [], []
    for which, order in enumerate(orders):
        sent, kept = gradients[2 * which : 2 * which + 2]
        shard = sent.shape[0] * sent.shape[1] // 2 ** (dev_bits - 1)
        split = (2,) * (dev_bits - 1) + (shard, sent.shape[2])
        parts = [kept.reshape(split), swap(sent, core_bit).reshape(split)]
        sums_of.append(Process(scatter_sum(parts, order, f32, given)))
    dmixed_slots[0] = after(dmixed_slots[0], w_triple, *given)
    early = [sums[i].reshape(n_dev, part) for i in range(6)] + [inner_sum.reshape(n_dev, -1)]

    dqkv_chunks, dqkv_slots, dqkv_parts, triples, late = [], [], [], [], []
    for chunk in range(chunks):
        dqkv, dqkv_placed = attention_backward(
            qkv, mixed_own[chunk], dmixed_slots, lse[chunk], where, chunk, chunks
        )
        if chunk < chunks - 1:
            slots = [dqkv[slot * rows : (slot + 1) * rows] for slot in range(n_ctx)]
            dqkv_slots += exchange_slots(slots)
            dmixed_slots[0] = after(dmixed_slots[0], *slots)
        else:
            dqkv_parts.append(lax.all_to_all(dqkv_placed, "ctx", 0, 0, tiled=True))
        dqkv_chunks.append(dqkv)

    together(sums_of, dqkv, *dqkv_slots)
    for one in sums_of:
        one.advance()
    for dqkv in dqkv_chunks:
        dqkv = after(dqkv, *given[-2:])
        grad_triple = lax.dot_general(
            tokens_all, dqkv, (((0,), (0,)), ((), ())), preferred_element_type=f32
        ).astype(bf16)
        triples.append(grad_triple.reshape((2,) * (dev_bits - ctx_bits) + (n_ctx, part, 384)))
        late.append(jnp.stack([row_sum(dqkv[:, :128]), row_sum(dqkv[:, 256:])]))
    triple_sum = jnp.concatenate(triples, axis=-1)
    half_sum = triple_sum.reshape((quads, 2) + triple_sum.shape[dev_bits - ctx_bits :])
    half_sum = Process(scatter_core(half_sum, core_bit))
    together(sums_of + [half_sum], *dqkv_parts)
    half_sum.advance()
    triple_sum = Process(scatter_at_once(half_sum.result, up_bits))
    for one in sums_of:
        one.advance()
    dqkv_parts = [after(part, *given[-2:]) for part in dqkv_parts]
    together([one for one in sums_of if one.result is None] + [triple_sum])
    triple_sum.advance()
    triple_sum = Process(exchange_line(triple_sum.result))
    for one in sums_of:
        one.advance()
    triple_sum = triple_sum.finish()
    grad_triple = triple_sum.reshape(n_ctx, part, chunks, 3, 128).transpose(3, 1, 0, 2, 4)
    grad_triple = grad_triple.reshape(3, part, width).astype(f32)
    grad_first, grad_outer = [one.finish() for one in sums_of]
    grad_attn, grad_inner = grad_first[:, :width], grad_first[:, width:]
    late = jnp.concatenate(late, axis=1)
    late = lax.dynamic_update_slice_in_dim(
        jnp.zeros((2, width), f32), late, place * group, 1
    )
    late = late.reshape(2, n_dev, part).transpose(1, 0, 2).reshape(n_dev, 2 * part)
    early = after(jnp.concatenate(early + [late], axis=1), *dqkv_parts)
    early = lax.all_to_all(early, AXES, 0, 0, tiled=True).sum(axis=0)
    late = early[early.shape[0] - 2 * part :].reshape(2, part)
    input_grad = input_gradient(where, dfirst, w_triple, dqkv_slots, dqkv_parts, n_ctx)

    pieces = [early[i * part : (i + 1) * part] for i in range(6)]
    return (
        layer_out,
        input_grad,
        grad_triple[0],
        late[0],
        grad_triple[1],
        grad_triple[2],
        late[1],
        grad_attn,
        pieces[3],
        pieces[4],
        pieces[5],
        grad_inner,
        early[6 * part : 6 * part + hidden_part],
        grad_outer,
        pieces[0],
        pieces[1],
        pieces[2],
    )


def solution(mesh):
    rows, vector = P(AXES, None), P(AXES)
    in_specs = (rows, P("dp"), rows, rows, vector, rows, rows, vector, rows) + (vector,) * 3
    in_specs += (rows, vector, rows) + (vector,) * 3
    out_specs = (rows,) * 3 + (vector, rows, rows, vector, rows) + (vector,) * 3
    out_specs += (rows, vector, rows) + (vector,) * 3
    return jax.shard_map(local, mesh=mesh, in_specs=in_specs, out_specs=out_specs, check_vma=False)
```

```python
import functools
import math

import jax
import jax.numpy as jnp
from jax import lax
from jax.experimental import pallas as pl
from jax.experimental.pallas import tpu as pltpu
from jax.sharding import PartitionSpec as P

HD = 64
AXES = ("dp", "ctx")
norm_eps = 1e-05
score_scale = 1.0 / math.sqrt(HD)
score_scale_two = score_scale * math.log2(math.e)
f32 = jnp.float32
bf16 = jnp.bfloat16


def kernel_cost(flops):
    return flops // 8


def attention_forward_kernel(
    place_ref, q_ref, k_ref, v_ref, mixed_ref, lse_ref, keys_t_ref, *, heads, rows
):
    width = k_ref.shape[1]
    seq = keys_t_ref.shape[1]

    @pl.when(pl.program_id(0) == 0)
    def _():
        keys_t_ref[...] = k_ref[...].T

    queries = q_ref[...]
    keys_t = keys_t_ref[...]
    values = v_ref[...]
    slots = [
        (place_ref[0] ^ slot) * rows + lax.broadcasted_iota(jnp.int32, (1, rows), 1)
        for slot in range(seq // rows)
    ]
    key_pos = jnp.concatenate(slots, axis=1)
    bias = jnp.where(key_pos < place_ref[1], 0.0, -1e30).astype(f32)
    head_of = lax.broadcasted_iota(jnp.int32, (rows, width), 1) // HD
    lane = lax.broadcasted_iota(jnp.int32, (rows, 128), 1)
    mixed = jnp.zeros((rows, width), f32)
    lse = jnp.zeros((rows, 128), f32)
    for head in range(heads):
        own = jnp.where(head_of == head, queries, jnp.zeros_like(queries))
        scores = jnp.dot(own, keys_t, preferred_element_type=f32) * score_scale_two + bias
        top = jnp.max(scores, axis=1, keepdims=True)
        probs = jnp.exp2(scores - top)
        total = jnp.sum(probs, axis=1, keepdims=True)
        part = jnp.dot(probs.astype(bf16), values, preferred_element_type=f32)
        mixed = jnp.where(head_of == head, part * (1.0 / total), mixed)
        lse = jnp.where(lane == head, top + jnp.log2(total), lse)
    mixed_ref[...] = mixed.astype(bf16)
    lse_ref[...] = lse.T[:8]


def attention_forward(qkv, place, rows, chunk, chunks):
    seq = qkv.shape[0]
    width = qkv.shape[1] // (3 * chunks)
    heads = width // HD
    return pl.pallas_call(
        functools.partial(attention_forward_kernel, heads=heads, rows=rows),
        grid=(seq // rows,),
        in_specs=[
            pl.BlockSpec(memory_space=pltpu.SMEM),
            pl.BlockSpec((rows, width), lambda i: (i, chunk)),
            pl.BlockSpec((seq, width), lambda i: (0, chunks + chunk)),
            pl.BlockSpec((seq, width), lambda i: (0, 2 * chunks + chunk)),
        ],
        out_specs=[
            pl.BlockSpec((rows, width), lambda i: (i, 0)),
            pl.BlockSpec((8, rows), lambda i: (0, i)),
        ],
        out_shape=[
            jax.ShapeDtypeStruct((seq, width), bf16),
            jax.ShapeDtypeStruct((8, seq), f32),
        ],
        scratch_shapes=[pltpu.VMEM((width, seq), bf16)],
        compiler_params=pltpu.CompilerParams(vmem_limit_bytes=56 * 2**20),
        cost_estimate=pl.CostEstimate(
            flops=kernel_cost(16 * seq * seq * width),
            bytes_accessed=8 * seq * width,
            transcendentals=seq * seq * heads,
        ),
        name="attention_forward",
    )(place, qkv, qkv, qkv)


def attention_backward_kernel(
    place_ref,
    q_ref,
    k_ref,
    v_ref,
    mixed_ref,
    lse_ref,
    *refs,
    heads,
    rows,
):
    step = pl.program_id(0)
    dmixed_refs, (out_ref, placed_ref, keys_t_ref, dk_sum, dv_sum, dmixed_ref) = refs[:-6], refs[-6:]
    seq, width = dk_sum.shape
    for slot, slot_ref in enumerate(dmixed_refs):

        @pl.when(step == slot)
        def _(slot_ref=slot_ref):
            dmixed_ref[...] = slot_ref[...]

    @pl.when(step == 0)
    def _():
        keys_t_ref[...] = k_ref[...].T
        dk_sum[...] = jnp.zeros_like(dk_sum)
        dv_sum[...] = jnp.zeros_like(dv_sum)

    queries, dmixed = q_ref[...], dmixed_ref[...]
    queries_t, dmixed_t, mixed_t = queries.T, dmixed.T, mixed_ref[...].T
    product = dmixed_t.astype(f32) * mixed_t.astype(f32)
    lane_head = lax.broadcasted_iota(jnp.int32, (rows, width), 1) // HD
    row_head = lax.broadcasted_iota(jnp.int32, (width, rows), 0) // HD
    none, none_t = jnp.zeros_like(queries), jnp.zeros_like(queries_t)
    lse = lse_ref[...]
    per_head = []
    for head in range(heads):
        per_head.append(
            (
                jnp.where(row_head == head, queries_t, none_t),
                jnp.where(row_head == head, dmixed_t, none_t),
                jnp.where(lane_head == head, queries, none),
                jnp.where(lane_head == head, dmixed, none),
                jnp.sum(product[HD * head : HD * head + HD], axis=0, keepdims=True),
                lse[head : head + 1],
            )
        )

    def chunk(index, dq_t):
        span = pl.ds(pl.multiple_of(index * rows, rows), rows)
        keys, values = k_ref[span, :], v_ref[span, :]
        key_pos = (place_ref[0] ^ index) * rows + lax.broadcasted_iota(jnp.int32, (rows, 1), 0)
        bias = jnp.where(key_pos < place_ref[1], 0.0, -1e30).astype(f32)
        dk, dv = dk_sum[span, :], dv_sum[span, :]
        new_dq_t = []
        for head in range(heads):
            own_q_t, own_do_t, own_q, own_do, delta, own_lse = per_head[head]
            scores = jnp.dot(keys, own_q_t, preferred_element_type=f32)
            probs = jnp.exp2(scores * score_scale_two + bias - own_lse)
            dprobs = jnp.dot(values, own_do_t, preferred_element_type=f32)
            dscores = (probs * (dprobs - delta)).astype(bf16)
            dv = dv + jnp.dot(probs.astype(bf16), own_do, preferred_element_type=f32)
            dk = dk + jnp.dot(dscores, own_q, preferred_element_type=f32)
            own_keys_t = keys_t_ref[HD * head : HD * head + HD, span]
            new_dq_t.append(
                dq_t[head] + jnp.dot(own_keys_t, dscores, preferred_element_type=f32)
            )
        dk_sum[span, :] = dk
        dv_sum[span, :] = dv
        return tuple(new_dq_t)

    start = tuple(jnp.zeros((HD, rows), f32) for _ in range(heads))
    dq_t = jnp.concatenate(lax.fori_loop(0, seq // rows, chunk, start, unroll=4), axis=0)
    own_rows = pl.ds(pl.multiple_of(step * rows, rows), rows)
    out_ref[own_rows, :width] = (dq_t * score_scale).T.astype(bf16)

    @pl.when(step == pl.num_programs(0) - 1)
    def _():
        out_ref[:, width : 2 * width] = (dk_sum[...] * score_scale).astype(bf16)
        out_ref[:, 2 * width :] = dv_sum[...].astype(bf16)
        for slot in range(seq // rows):
            placed_ref[place_ref[0] ^ slot] = out_ref[slot * rows : (slot + 1) * rows, :]


def attention_backward(qkv, mixed, dmixed_slots, lse, place, chunk, chunks):
    seq, width = mixed.shape
    rows = seq // len(dmixed_slots)
    heads = width // HD
    block = pl.BlockSpec((rows, width), lambda i: (i, 0))
    return pl.pallas_call(
        functools.partial(attention_backward_kernel, heads=heads, rows=rows),
        grid=(seq // rows,),
        in_specs=[
            pl.BlockSpec(memory_space=pltpu.SMEM),
            pl.BlockSpec((rows, width), lambda i: (i, chunk)),
            pl.BlockSpec((seq, width), lambda i: (0, chunks + chunk)),
            pl.BlockSpec((seq, width), lambda i: (0, 2 * chunks + chunk)),
            block,
            pl.BlockSpec((8, rows), lambda i: (0, i)),
        ]
        + [pl.BlockSpec((rows, width), lambda i: (0, chunk))] * len(dmixed_slots),
        out_specs=[
            pl.BlockSpec((seq, 3 * width), lambda i: (0, 0)),
            pl.BlockSpec((seq // rows, rows, 3 * width), lambda i: (0, 0, 0)),
        ],
        out_shape=[
            jax.ShapeDtypeStruct((seq, 3 * width), bf16),
            jax.ShapeDtypeStruct((seq // rows, rows, 3 * width), bf16),
        ],
        scratch_shapes=[
            pltpu.VMEM((width, seq), bf16),
            pltpu.VMEM((seq, width), f32),
            pltpu.VMEM((seq, width), f32),
            pltpu.VMEM((rows, width), bf16),
        ],
        compiler_params=pltpu.CompilerParams(vmem_limit_bytes=56 * 2**20),
        cost_estimate=pl.CostEstimate(
            flops=kernel_cost(40 * seq * seq * width),
            bytes_accessed=16 * seq * width,
            transcendentals=seq * seq * heads,
        ),
        name="attention_backward",
    )(place, qkv, qkv, qkv, mixed, lse, *dmixed_slots)


def layer_kernel(
    place_ref,
    tokens_ref,
    cotangent_ref,
    vectors_ref,
    inner_offset_ref,
    *refs,
    chunks,
    groups,
):
    mixed_refs, refs = refs[: chunks * groups], refs[chunks * groups :]
    weight_refs, refs = refs[:2], refs[2:]
    (layer_out_ref, dfirst_ref, sums_ref, inner_sum_ref), refs = refs[:4], refs[4:]
    dmixed_refs, gradient_refs, refs = refs[:groups], refs[groups : groups + 4], refs[groups + 4 :]
    (w_attn, w_inner, w_outer), refs = refs[:3], refs[3:]
    (mixed_ref, hidden_ref, act_ref, douter_ref, dpre_ref, dattn_ref), refs = refs[:6], refs[6:]
    (wide_ref, normed_ref, inverse_ref, total_ref, dmixed_ref, turned_ref, sems) = refs
    rows, width = tokens_ref.shape
    hidden_width = w_inner.shape[1]
    place, length, core, quad = place_ref[0], place_ref[1], place_ref[2], place_ref[3]
    first_row = place * rows

    first_weights, outer_weights = weight_refs
    copies = [
        pltpu.make_async_copy(first_weights.at[:, :width], w_attn, sems.at[0]),
        pltpu.make_async_copy(first_weights.at[:, width:], w_inner, sems.at[1]),
        pltpu.make_async_copy(outer_weights, w_outer, sems.at[2]),
    ]
    for copy in copies:
        copy.start()

    b_attn, g_attn, s_attn = vectors_ref[0:1], vectors_ref[1:2], vectors_ref[2:3]
    b_outer, g_final, s_final = vectors_ref[3:4], vectors_ref[4:5], vectors_ref[5:6]
    chunk_width = mixed_refs[0].shape[1]

    def columns_of(chunk, slot):
        start = ((place ^ slot) * chunks + chunk) * chunk_width
        return pl.ds(pl.multiple_of(start, chunk_width), chunk_width)

    for chunk in range(chunks):
        for slot in range(groups):
            mixed_ref[:, columns_of(chunk, slot)] = mixed_refs[chunk * groups + slot][...]

    copies[0].wait()

    step = 128

    def norm_one(turn, carried):
        span = pl.ds(pl.multiple_of(turn * step, step), step)
        first = (
            tokens_ref[span, :].astype(f32)
            + jnp.dot(mixed_ref[span, :], w_attn[...], preferred_element_type=f32)
            + b_attn
        )
        centered = first - jnp.mean(first, axis=1, keepdims=True)
        inverse = lax.rsqrt(jnp.mean(centered * centered, axis=1, keepdims=True) + norm_eps)
        normed = centered * inverse
        hidden = normed * g_attn + s_attn
        normed_ref[span, :] = normed
        inverse_ref[span, :] = jnp.broadcast_to(inverse, (step, 128))
        total_ref[span, :] = hidden
        hidden_ref[span, :] = hidden.astype(bf16)
        return carried

    lax.fori_loop(0, rows // step, norm_one, 0, unroll=2)

    copies[1].wait()
    block = 512

    def feed_in(turn, carried):
        span = pl.ds(pl.multiple_of(turn * block, block), block)
        pre = (
            jnp.dot(hidden_ref[...], w_inner[:, span], preferred_element_type=f32)
            + inner_offset_ref[:, span]
        )
        normal_cdf = 0.5 * (1.0 + lax.erf(pre * (1.0 / math.sqrt(2.0))))
        act_ref[:, span] = (pre * normal_cdf).astype(bf16)
        slope = normal_cdf + pre * jnp.exp(-0.5 * pre * pre) * (1.0 / math.sqrt(2.0 * math.pi))
        dpre_ref[:, span] = slope.astype(bf16)
        return carried

    lax.fori_loop(0, hidden_width // block, feed_in, 0, unroll=4)

    copies[2].wait()
    narrow = 512

    def feed_out(turn, carried):
        span = pl.ds(pl.multiple_of(turn * narrow, narrow), narrow)
        wide_ref[:, span] = jnp.dot(act_ref[...], w_outer[:, span], preferred_element_type=f32)
        return carried

    lax.fori_loop(0, width // narrow, feed_out, 0, unroll=2)

    def norm_two(turn, carried):
        span = pl.ds(pl.multiple_of(turn * step, step), step)
        second = total_ref[span, :] + wide_ref[span, :] + b_outer
        centered = second - jnp.mean(second, axis=1, keepdims=True)
        inverse = lax.rsqrt(jnp.mean(centered * centered, axis=1, keepdims=True) + norm_eps)
        normed = centered * inverse
        row = first_row + turn * step + lax.broadcasted_iota(jnp.int32, (step, 1), 0)
        valid = jnp.where(row < length, 1.0, 0.0).astype(f32)
        layer_out_ref[span, :] = ((normed * g_final + s_final) * valid).astype(bf16)
        upstream = cotangent_ref[span, :].astype(f32) * valid
        shift_sum, gain_sum, offset_sum = carried
        shift_sum = shift_sum + jnp.sum(upstream, axis=0, keepdims=True)
        gain_sum = gain_sum + jnp.sum(upstream * normed, axis=0, keepdims=True)
        scaled = upstream * g_final
        first_mean = jnp.mean(scaled, axis=1, keepdims=True)
        second_mean = jnp.mean(scaled * normed, axis=1, keepdims=True)
        dsecond = inverse * (scaled - first_mean - normed * second_mean)
        total_ref[span, :] = dsecond
        douter = dsecond.astype(bf16)
        douter_ref[span, :] = douter
        offset_sum = offset_sum + jnp.sum(douter.astype(f32), axis=0, keepdims=True)
        return (shift_sum, gain_sum, offset_sum)

    none = jnp.zeros((1, width), f32)
    shift_sum, gain_sum, offset_sum = lax.fori_loop(
        0, rows // step, norm_two, (none, none, none), unroll=2
    )
    sums_ref[0:1] = offset_sum
    sums_ref[1:2] = gain_sum
    sums_ref[2:3] = shift_sum

    across = (((1,), (1,)), ((), ()))

    def back_out(turn, carried):
        span = pl.ds(pl.multiple_of(turn * block, block), block)
        dact = lax.dot_general(
            douter_ref[...], w_outer[span, :], across, preferred_element_type=f32
        )
        dpre = (dact * dpre_ref[:, span].astype(f32)).astype(bf16)
        dpre_ref[:, span] = dpre
        inner_sum_ref[:, span] = jnp.sum(dpre.astype(f32), axis=0, keepdims=True)
        return carried

    lax.fori_loop(0, hidden_width // block, back_out, 0, unroll=4)

    quads = gradient_refs[0].shape[0]
    slab, outer_slab = width // (2 * quads), hidden_width // (2 * quads)
    down = (((0,), (0,)), ((), ()))

    def leave(first_sem, source, which, to_col, height):
        started = []
        levels = quads.bit_length() - 1
        if which == 0:
            order = [
                sum(((slot >> i) & 1) << (levels - 1 - i) for i in range(levels))
                for slot in range(quads)
            ]
        else:
            order = list(range(quads))
        for side in range(2):
            owner = 1 - core if side == 0 else core
            for slot in range(quads):
                row = pl.multiple_of((2 * (order[slot] ^ quad) + owner) * height, height)
                copy = pltpu.make_async_copy(
                    source.at[pl.ds(row, height), :],
                    gradient_refs[2 * which + side].at[slot, :, to_col : to_col + source.shape[1]],
                    sems.at[first_sem + len(started)],
                )
                copy.start()
                started.append(copy)
        return started

    def outer_gradient(turn, carried):
        span = pl.ds(pl.multiple_of(turn * block, block), block)
        terms = lax.dot_general(
            act_ref[:, span], douter_ref[...], down, preferred_element_type=f32
        )
        w_outer[span, :] = terms.astype(bf16)
        return carried

    lax.fori_loop(0, hidden_width // block, outer_gradient, 0, unroll=2)
    leaving = leave(3, w_outer, 1, 0, outer_slab)

    def back_in(turn, carried):
        span = pl.ds(pl.multiple_of(turn * narrow, narrow), narrow)
        wide_ref[:, span] = lax.dot_general(
            dpre_ref[...], w_inner[span, :], across, preferred_element_type=f32
        )
        return carried

    lax.fori_loop(0, width // narrow, back_in, 0, unroll=2)

    def norm_one_back(turn, carried):
        span = pl.ds(pl.multiple_of(turn * step, step), step)
        dhidden = total_ref[span, :] + wide_ref[span, :]
        normed = normed_ref[span, :]
        inverse = inverse_ref[span, 0:1]
        shift_sum, gain_sum, offset_sum = carried
        shift_sum = shift_sum + jnp.sum(dhidden, axis=0, keepdims=True)
        gain_sum = gain_sum + jnp.sum(dhidden * normed, axis=0, keepdims=True)
        scaled = dhidden * g_attn
        first_mean = jnp.mean(scaled, axis=1, keepdims=True)
        second_mean = jnp.mean(scaled * normed, axis=1, keepdims=True)
        dfirst = inverse * (scaled - first_mean - normed * second_mean)
        dfirst_ref[span, :] = dfirst
        dattn = dfirst.astype(bf16)
        dattn_ref[span, :] = dattn
        offset_sum = offset_sum + jnp.sum(dattn.astype(f32), axis=0, keepdims=True)
        dmixed = lax.dot_general(dattn, w_attn[...], across, preferred_element_type=f32)
        dmixed_ref[span, :] = dmixed.astype(bf16)
        return (shift_sum, gain_sum, offset_sum)

    shift_sum, gain_sum, offset_sum = lax.fori_loop(
        0, rows // step, norm_one_back, (none, none, none), unroll=2
    )
    sums_ref[3:4] = offset_sum
    sums_ref[4:5] = gain_sum
    sums_ref[5:6] = shift_sum
    sums_ref[6:8] = jnp.zeros((2, width), f32)
    group_width = chunks * chunk_width
    for slot in range(groups):
        start = pl.multiple_of((place ^ slot) * group_width, group_width)
        dmixed_refs[slot][...] = dmixed_ref[:, pl.ds(start, group_width)]

    turned_ref[...] = hidden_ref[...].T
    wide_block = 1024

    def inner_gradient(turn, carried):
        span = pl.ds(pl.multiple_of(turn * wide_block, wide_block), wide_block)
        for half in range(width // block):
            rows_of = slice(half * block, (half + 1) * block)
            terms = jnp.dot(turned_ref[rows_of, :], dpre_ref[:, span], preferred_element_type=f32)
            w_inner[rows_of, span] = terms.astype(bf16)
        return carried

    lax.fori_loop(0, hidden_width // wide_block, inner_gradient, 0, unroll=2)
    leaving += leave(3 + len(leaving), w_inner, 0, width, slab)
    turned_ref[...] = mixed_ref[...].T
    for half in range(width // block):
        rows_of = slice(half * block, (half + 1) * block)
        terms = jnp.dot(turned_ref[rows_of, :], dattn_ref[...], preferred_element_type=f32)
        w_attn[rows_of, :] = terms.astype(bf16)
    leaving += leave(3 + len(leaving), w_attn, 0, 0, slab)
    for copy in leaving:
        copy.wait()


def layer_middle(place, tokens, cotangent, vectors, inner_offset, mixed_parts, groups, weights, quads):
    rows, width = tokens.shape
    hidden_width = inner_offset.shape[1]
    chunk_width = mixed_parts[0].shape[1]
    chunks = len(mixed_parts) // groups
    slab, outer_slab = width // (2 * quads), hidden_width // (2 * quads)
    vmem = pl.BlockSpec(memory_space=pltpu.VMEM)
    anywhere = pl.BlockSpec(memory_space=pl.ANY)
    shapes = [
        jax.ShapeDtypeStruct((rows, width), bf16),
        jax.ShapeDtypeStruct((rows, width), f32),
        jax.ShapeDtypeStruct((8, width), f32),
        jax.ShapeDtypeStruct((1, hidden_width), f32),
    ] + [jax.ShapeDtypeStruct((rows, chunks * chunk_width), bf16)] * groups
    gradients = [
        jax.ShapeDtypeStruct((quads, slab, width + hidden_width), bf16),
        jax.ShapeDtypeStruct((quads, outer_slab, width), bf16),
    ]
    gradients = [shape for shape in gradients for _ in range(2)]
    return pl.pallas_call(
        functools.partial(layer_kernel, chunks=chunks, groups=groups),
        in_specs=[pl.BlockSpec(memory_space=pltpu.SMEM)]
        + [vmem] * (4 + chunks * groups)
        + [anywhere] * 2,
        out_specs=[vmem] * len(shapes) + [anywhere] * 4,
        out_shape=shapes + gradients,
        scratch_shapes=[
            pltpu.VMEM((width, width), bf16),
            pltpu.VMEM((width, hidden_width), bf16),
            pltpu.VMEM((hidden_width, width), bf16),
            pltpu.VMEM((rows, width), bf16),
            pltpu.VMEM((rows, width), bf16),
            pltpu.VMEM((rows, hidden_width), bf16),
            pltpu.VMEM((rows, width), bf16),
            pltpu.VMEM((rows, hidden_width), bf16),
            pltpu.VMEM((rows, width), bf16),
            pltpu.VMEM((rows, width), f32),
            pltpu.VMEM((rows, width), f32),
            pltpu.VMEM((rows, 128), f32),
            pltpu.VMEM((rows, width), f32),
            pltpu.VMEM((rows, width), bf16),
            pltpu.VMEM((width, rows), bf16),
            pltpu.SemaphoreType.DMA((3 + 6 * quads,)),
        ],
        compiler_params=pltpu.CompilerParams(vmem_limit_bytes=60 * 2**20),
        cost_estimate=pl.CostEstimate(
            flops=kernel_cost(12 * rows * width * (hidden_width + width)),
            bytes_accessed=4 * width * (2 * hidden_width + width) + 10 * rows * width,
            transcendentals=2 * rows * hidden_width,
        ),
        name="layer_middle",
    )(place, tokens, cotangent, vectors, inner_offset, *mixed_parts, *weights)


def input_kernel(place_ref, dfirst_ref, weights_ref, *refs, slotted, placed, groups):
    slots, parts, (out_ref, rows_ref) = refs[:slotted], refs[slotted:-2], refs[-2:]
    cols = weights_ref.shape[1] // (groups * (slotted // groups + placed))
    chunk = 0
    for first in range(0, slotted, groups):
        for slot in range(groups):
            start = (chunk * groups + (place_ref[0] ^ slot)) * cols
            span = pl.ds(pl.multiple_of(start, cols), cols)
            rows_ref[:, span] = slots[first + slot][...]
        chunk += 1
    for part in parts:
        for group in range(groups):
            start = (chunk * groups + group) * cols
            rows_ref[:, start : start + cols] = part[group]
        chunk += 1
    block = 512

    def columns(turn, carried):
        span = pl.ds(pl.multiple_of(turn * block, block), block)
        terms = lax.dot_general(
            rows_ref[...],
            weights_ref[span, :],
            (((1,), (1,)), ((), ())),
            preferred_element_type=f32,
        )
        out_ref[:, span] = (dfirst_ref[:, span] + terms).astype(bf16)
        return carried

    lax.fori_loop(0, out_ref.shape[1] // block, columns, 0)


def input_gradient(place, dfirst, weights, slots, parts, groups):
    rows, width = dfirst.shape
    vmem = pl.BlockSpec(memory_space=pltpu.VMEM)
    given = list(slots) + list(parts)
    return pl.pallas_call(
        functools.partial(input_kernel, slotted=len(slots), placed=len(parts), groups=groups),
        in_specs=[pl.BlockSpec(memory_space=pltpu.SMEM)] + [vmem] * (2 + len(given)),
        out_specs=vmem,
        out_shape=jax.ShapeDtypeStruct((rows, width), bf16),
        scratch_shapes=[pltpu.VMEM((rows, weights.shape[1]), bf16)],
        compiler_params=pltpu.CompilerParams(vmem_limit_bytes=48 * 2**20),
        cost_estimate=pl.CostEstimate(
            flops=kernel_cost(2 * rows * width * weights.shape[1]),
            bytes_accessed=2 * width * weights.shape[1] + 12 * rows * width,
            transcendentals=0,
        ),
        name="input_gradient",
    )(place, dfirst, weights, *given)


def device_index():
    return lax.axis_index("dp") * lax.axis_size("ctx") + lax.axis_index("ctx")


def bits_of(count):
    return count.bit_length() - 1


def swap(values, bit):
    count = lax.axis_size("dp") * lax.axis_size("ctx")
    return lax.ppermute(values, AXES, [(i, i ^ (1 << bit)) for i in range(count)])


def own_bit(bit):
    return (device_index() >> bit) & 1


def joined(shard, other, bit, axis):
    return jnp.where(
        own_bit(bit) == 1,
        jnp.stack([other, shard], axis=axis),
        jnp.stack([shard, other], axis=axis),
    )


def after(value, *others):
    return lax.optimization_barrier((value,) + others)[0]


def gather_line(block):
    count = lax.axis_size("ctx")
    place = lax.axis_index("ctx")
    held = jnp.broadcast_to(block[None], (count,) + block.shape)
    from_left = from_right = block
    for step in range(1, count):
        from_left, from_right = yield [
            lax.ppermute(from_left, "ctx", [(i, i + 1) for i in range(count - 1)]),
            lax.ppermute(from_right, "ctx", [(i + 1, i) for i in range(count - 1)]),
        ]
        for arrived, source in ((from_left, place - step), (from_right, place + step)):
            inside = (source >= 0) & (source < count)
            held = lax.dynamic_update_index_in_dim(
                held,
                jnp.where(inside, arrived, block),
                jnp.where(inside, source ^ place, 0),
                0,
            )
    return held.reshape((count * block.shape[0],) + block.shape[1:])


def exchange_slots(slots):
    count = lax.axis_size("ctx")
    return [slots[0]] + [
        lax.ppermute(slots[mask], "ctx", [(i, i ^ mask) for i in range(count)])
        for mask in range(1, count)
    ]


def exchange_line(blocks):
    count = lax.axis_size("ctx")
    place = lax.axis_index("ctx")
    arrived = yield [
        lax.ppermute(
            lax.dynamic_index_in_dim(blocks, place ^ mask, 0, keepdims=False),
            "ctx",
            [(i, i ^ mask) for i in range(count)],
        )
        for mask in range(1, count)
    ]
    for mask, value in enumerate(arrived, 1):
        blocks = lax.dynamic_update_index_in_dim(blocks, value, place ^ mask, 0)
    return blocks


def gather_bits(shard, bit_order):
    held = []
    for bit in bit_order:
        (other,) = yield [swap(shard, bit)]
        held = sorted(held + [bit], reverse=True)
        shard = joined(shard, other, bit, held.index(bit))
    return shard.reshape((2 ** len(held),) + shard.shape[len(held) :])


def gather_group(packed, bit_order):
    packed = yield from exchange_line(packed)
    return (yield from gather_bits(packed, bit_order))


def scatter_sum(parts, bit_order, out_dtype, sent):
    left = sorted([bit for bit in bit_order if bit < bits_of(lax.axis_size("ctx"))], reverse=True)
    for bit in bit_order:
        if bit not in left:
            given, parts = [part[1] for part in parts], [part[0] for part in parts]
        else:
            axis, mine = left.index(bit), own_bit(bit)
            given = [lax.dynamic_index_in_dim(part, 1 - mine, axis, False) for part in parts]
            parts = [lax.dynamic_index_in_dim(part, mine, axis, False) for part in parts]
        if bit == bit_order[0]:
            given, kept = total_of(given, parts[0].dtype), total_of(parts, parts[0].dtype)
        else:
            given, kept = given[0] + given[1], parts[0] + parts[1]
        sent.append(given)
        parts = [kept] + (yield [swap(given, bit)])
        if bit in left:
            left.remove(bit)
    return total_of(parts, out_dtype)


def total_of(parts, dtype):
    total = parts[0].astype(f32)
    for part in parts[1:]:
        total = total + part.astype(f32)
    return total.astype(dtype)


def scatter_core(terms, bit):
    mine = own_bit(bit)
    (received,) = yield [swap(lax.dynamic_index_in_dim(terms, 1 - mine, 1, False), bit)]
    kept = lax.dynamic_index_in_dim(terms, mine, 1, False)
    return total_of([kept, received], terms.dtype)


def scatter_at_once(terms, bits):
    masks = range(1, 2 ** len(bits))
    low = min(bits)
    place = (device_index() >> low) & (2 ** len(bits) - 1)
    count = lax.axis_size("dp") * lax.axis_size("ctx")
    received = yield [
        lax.ppermute(
            lax.dynamic_index_in_dim(terms, place ^ mask, 0, keepdims=False),
            AXES,
            [(i, i ^ (mask << low)) for i in range(count)],
        )
        for mask in masks
    ]
    total = lax.dynamic_index_in_dim(terms, place, 0, keepdims=False).astype(f32)
    for value in received:
        total = total + value.astype(f32)
    return total.astype(terms.dtype)


class Process:
    def __init__(self, process):
        self.process = process
        self.arrived = next(process)
        self.result = None

    def advance(self):
        if self.result is not None:
            return
        try:
            self.arrived = self.process.send(self.arrived)
        except StopIteration as stop:
            self.arrived, self.result = [], stop.value

    def finish(self):
        while self.result is None:
            self.advance()
        return self.result


def together(processes, *others):
    flat = [value for process in processes for value in process.arrived]
    flat = list(lax.optimization_barrier(tuple(flat) + tuple(others)))
    for process in processes:
        count = len(process.arrived)
        process.arrived, flat = flat[:count], flat[count:]


def row_sum(values):
    return jnp.sum(values.astype(f32), axis=0)


def local(
    tokens,
    lengths,
    cotangent,
    query_proj,
    query_offset,
    key_proj,
    value_proj,
    value_offset,
    attn_proj,
    attn_offset,
    attn_gain,
    attn_shift,
    inner_proj,
    inner_offset,
    outer_proj,
    outer_offset,
    final_gain,
    final_shift,
):
    n_dp, n_ctx = lax.axis_size("dp"), lax.axis_size("ctx")
    n_dev = n_dp * n_ctx
    dev_bits = bits_of(n_dev)
    ctx_bits = bits_of(n_ctx)
    rows, width = tokens.shape
    seq = rows * n_ctx
    group = width // n_ctx
    part = width // n_dev
    hidden_width = inner_proj.shape[1]
    hidden_part = hidden_width // n_dev
    chunks = group // 128
    place = lax.axis_index("ctx")
    core_bit = ctx_bits
    up_bits = list(range(ctx_bits + 1, dev_bits))
    down_bits = up_bits[::-1]
    ctx_down = list(range(ctx_bits))[::-1]
    ctx_up = list(range(ctx_bits))

    vectors = jnp.concatenate(
        [
            query_offset,
            value_offset,
            attn_offset,
            attn_gain,
            attn_shift,
            outer_offset,
            final_gain,
            final_shift,
            inner_offset,
        ]
    ).astype(bf16)
    triple = jnp.stack([query_proj, key_proj, value_proj], axis=1).astype(bf16)
    by_group = triple.reshape(part, 3, n_ctx, group).transpose(2, 0, 1, 3)
    by_group = by_group.reshape(n_ctx, part, 3 * group)
    vector_rows = -(-vectors.shape[0] // (3 * group))
    vectors = jnp.pad(vectors, (0, vector_rows * 3 * group - vectors.shape[0]))
    vectors = vectors.reshape(vector_rows, 3 * group)
    vectors = jnp.pad(vectors, ((0, 16 - vector_rows), (0, 0)))
    packed = jnp.concatenate(
        [by_group, jnp.broadcast_to(vectors[None], (n_ctx,) + vectors.shape)], axis=1
    )

    first_shard = jnp.concatenate([attn_proj, inner_proj], axis=1).astype(bf16)
    w_first = lax.all_gather(first_shard, AXES, axis=0, tiled=True)
    w_outer = lax.all_gather(outer_proj.astype(bf16), AXES, axis=0, tiled=True)
    line = Process(gather_line(tokens))
    projections = Process(gather_group(packed, down_bits + [core_bit]))
    for turn in range(n_ctx - 1):
        together([line, projections])
        line.advance()
        projections.advance()
    tokens_all, packed = line.result, projections.finish()
    w_group = packed[:, :, :part].reshape(width, 3 * group)
    vectors = packed[:, :, part : part + vector_rows].reshape(n_dev, -1)
    names = [vectors[:, i * part : (i + 1) * part].reshape(width).astype(f32) for i in range(8)]
    b_query, b_value, b_attn, g_attn, s_attn, b_outer, g_final, s_final = names
    b_inner = vectors[:, 8 * part : 8 * part + hidden_part].reshape(1, hidden_width).astype(f32)

    b_group = lax.dynamic_slice_in_dim(
        jnp.stack([b_query, jnp.zeros_like(b_query), b_value]), place * group, group, 1
    ).reshape(3 * group)
    qkv = (jnp.dot(tokens_all, w_group, preferred_element_type=f32) + b_group).astype(bf16)
    where = jnp.stack(
        [place, lengths[0], own_bit(core_bit), lax.axis_index("dp") // 2]
    ).astype(jnp.int32)
    mixed_own, lse, mixed_parts = [], [], []
    for chunk in range(chunks):
        mixed_chunk, lse_chunk = attention_forward(qkv, where, rows, chunk, chunks)
        mixed_own.append(mixed_chunk)
        lse.append(lse_chunk)
        mixed_parts += exchange_slots(
            [mixed_chunk[slot * rows : (slot + 1) * rows] for slot in range(n_ctx)]
        )

    by_chunk = triple.reshape(part, 3, n_ctx, chunks, 128).transpose(0, 3, 2, 1, 4)
    by_chunk = by_chunk.reshape(part, 3 * width)
    by_chunk, _ = lax.optimization_barrier((by_chunk, qkv))
    w_triple = lax.all_gather(by_chunk, AXES, axis=0, tiled=True)
    none = jnp.zeros_like(b_attn)
    layer_vectors = jnp.stack([b_attn, g_attn, s_attn, b_outer, g_final, s_final, none, none])
    quads = n_dp // 2
    middle = layer_middle(
        where,
        tokens,
        cotangent,
        layer_vectors,
        b_inner,
        mixed_parts,
        n_ctx,
        (w_first, w_outer),
        quads,
    )
    layer_out, dfirst, sums, inner_sum = middle[:4]
    dmixed_slots = exchange_slots(middle[4 : 4 + n_ctx])

    gradients = middle[4 + n_ctx :]
    orders = (
        up_bits + ctx_up,
        down_bits + ctx_down,
    )
    sums_of, given = [], []
    for which, order in enumerate(orders):
        sent, kept = gradients[2 * which : 2 * which + 2]
        shard = sent.shape[0] * sent.shape[1] // 2 ** (dev_bits - 1)
        split = (2,) * (dev_bits - 1) + (shard, sent.shape[2])
        parts = [kept.reshape(split), swap(sent, core_bit).reshape(split)]
        sums_of.append(Process(scatter_sum(parts, order, f32, given)))
    dmixed_slots[0] = after(dmixed_slots[0], w_triple, *given)
    early = [sums[i].reshape(n_dev, part) for i in range(6)] + [inner_sum.reshape(n_dev, -1)]

    dqkv_chunks, dqkv_slots, dqkv_parts, triples, late = [], [], [], [], []
    for chunk in range(chunks):
        dqkv, dqkv_placed = attention_backward(
            qkv, mixed_own[chunk], dmixed_slots, lse[chunk], where, chunk, chunks
        )
        if chunk < chunks - 1:
            slots = [dqkv[slot * rows : (slot + 1) * rows] for slot in range(n_ctx)]
            dqkv_slots += exchange_slots(slots)
            dmixed_slots[0] = after(dmixed_slots[0], *slots)
        else:
            dqkv_parts.append(lax.all_to_all(dqkv_placed, "ctx", 0, 0, tiled=True))
        dqkv_chunks.append(dqkv)

    together(sums_of, dqkv, *dqkv_slots)
    for one in sums_of:
        one.advance()
    for dqkv in dqkv_chunks:
        dqkv = after(dqkv, *given[-2:])
        grad_triple = lax.dot_general(
            tokens_all, dqkv, (((0,), (0,)), ((), ())), preferred_element_type=f32
        ).astype(bf16)
        triples.append(grad_triple.reshape((2,) * (dev_bits - ctx_bits) + (n_ctx, part, 384)))
        late.append(jnp.stack([row_sum(dqkv[:, :128]), row_sum(dqkv[:, 256:])]))
    triple_sum = jnp.concatenate(triples, axis=-1)
    half_sum = triple_sum.reshape((quads, 2) + triple_sum.shape[dev_bits - ctx_bits :])
    half_sum = Process(scatter_core(half_sum, core_bit))
    together(sums_of + [half_sum], *dqkv_parts)
    half_sum.advance()
    triple_sum = Process(scatter_at_once(half_sum.result, up_bits))
    for one in sums_of:
        one.advance()
    dqkv_parts = [after(part, *given[-2:]) for part in dqkv_parts]
    together([one for one in sums_of if one.result is None] + [triple_sum])
    triple_sum.advance()
    triple_sum = Process(exchange_line(triple_sum.result))
    for one in sums_of:
        one.advance()
    triple_sum = triple_sum.finish()
    grad_triple = triple_sum.reshape(n_ctx, part, chunks, 3, 128).transpose(3, 1, 0, 2, 4)
    grad_triple = grad_triple.reshape(3, part, width).astype(f32)
    grad_first, grad_outer = [one.finish() for one in sums_of]
    grad_attn, grad_inner = grad_first[:, :width], grad_first[:, width:]
    late = jnp.concatenate(late, axis=1)
    late = lax.dynamic_update_slice_in_dim(
        jnp.zeros((2, width), f32), late, place * group, 1
    )
    late = late.reshape(2, n_dev, part).transpose(1, 0, 2).reshape(n_dev, 2 * part)
    early = after(jnp.concatenate(early + [late], axis=1), *dqkv_parts)
    early = lax.all_to_all(early, AXES, 0, 0, tiled=True).sum(axis=0)
    late = early[early.shape[0] - 2 * part :].reshape(2, part)
    input_grad = input_gradient(where, dfirst, w_triple, dqkv_slots, dqkv_parts, n_ctx)

    pieces = [early[i * part : (i + 1) * part] for i in range(6)]
    return (
        layer_out,
        input_grad,
        grad_triple[0],
        late[0],
        grad_triple[1],
        grad_triple[2],
        late[1],
        grad_attn,
        pieces[3],
        pieces[4],
        pieces[5],
        grad_inner,
        early[6 * part : 6 * part + hidden_part],
        grad_outer,
        pieces[0],
        pieces[1],
        pieces[2],
    )


def solution(mesh):
    rows, vector = P(AXES, None), P(AXES)
    in_specs = (rows, P("dp"), rows, rows, vector, rows, rows, vector, rows) + (vector,) * 3
    in_specs += (rows, vector, rows) + (vector,) * 3
    out_specs = (rows,) * 3 + (vector, rows, rows, vector, rows) + (vector,) * 3
    out_specs += (rows, vector, rows) + (vector,) * 3
    return jax.shard_map(local, mesh=mesh, in_specs=in_specs, out_specs=out_specs, check_vma=False)
```

```python
import functools
import math

import jax
import jax.numpy as jnp
from jax import lax
from jax.experimental import pallas as pl
from jax.experimental.pallas import tpu as pltpu
from jax.sharding import PartitionSpec as P

HD = 64
AXES = ("dp", "ctx")
norm_eps = 1e-05
score_scale = 1.0 / math.sqrt(HD)
score_scale_two = score_scale * math.log2(math.e)
f32 = jnp.float32
bf16 = jnp.bfloat16


def kernel_cost(flops):
    return flops // 8


def attention_forward_kernel(
    place_ref, q_ref, k_ref, v_ref, mixed_ref, lse_ref, *refs, heads, rows
):
    slot_refs, keys_t_ref = refs[:-1], refs[-1]
    width = k_ref.shape[1]
    seq = keys_t_ref.shape[1]

    @pl.when(pl.program_id(0) == 0)
    def _():
        keys_t_ref[...] = k_ref[...].T

    queries = q_ref[...]
    keys_t = keys_t_ref[...]
    values = v_ref[...]
    slots = [
        (place_ref[0] ^ slot) * rows + lax.broadcasted_iota(jnp.int32, (1, rows), 1)
        for slot in range(seq // rows)
    ]
    key_pos = jnp.concatenate(slots, axis=1)
    bias = jnp.where(key_pos < place_ref[1], 0.0, -1e30).astype(f32)
    head_of = lax.broadcasted_iota(jnp.int32, (rows, width), 1) // HD
    lane = lax.broadcasted_iota(jnp.int32, (rows, 128), 1)
    mixed = jnp.zeros((rows, width), f32)
    lse = jnp.zeros((rows, 128), f32)
    for head in range(heads):
        own = jnp.where(head_of == head, queries, jnp.zeros_like(queries))
        scores = jnp.dot(own, keys_t, preferred_element_type=f32) * score_scale_two + bias
        top = jnp.max(scores, axis=1, keepdims=True)
        probs = jnp.exp2(scores - top)
        total = jnp.sum(probs, axis=1, keepdims=True)
        part = jnp.dot(probs.astype(bf16), values, preferred_element_type=f32)
        mixed = jnp.where(head_of == head, part * (1.0 / total), mixed)
        lse = jnp.where(lane == head, top + jnp.log2(total), lse)
    mixed_ref[...] = mixed.astype(bf16)
    for slot, slot_ref in enumerate(slot_refs):

        @pl.when(pl.program_id(0) == slot)
        def _(slot_ref=slot_ref):
            slot_ref[...] = mixed_ref[...]

    lse_ref[...] = lse.T[:8]


def attention_forward(qkv, place, rows, chunk, chunks):
    seq = qkv.shape[0]
    width = qkv.shape[1] // (3 * chunks)
    heads = width // HD
    return pl.pallas_call(
        functools.partial(attention_forward_kernel, heads=heads, rows=rows),
        grid=(seq // rows,),
        in_specs=[
            pl.BlockSpec(memory_space=pltpu.SMEM),
            pl.BlockSpec((rows, width), lambda i: (i, chunk)),
            pl.BlockSpec((seq, width), lambda i: (0, chunks + chunk)),
            pl.BlockSpec((seq, width), lambda i: (0, 2 * chunks + chunk)),
        ],
        out_specs=[
            pl.BlockSpec((rows, width), lambda i: (i, 0)),
            pl.BlockSpec((8, rows), lambda i: (0, i)),
        ]
        + [pl.BlockSpec((rows, width), lambda i: (0, 0))] * (seq // rows),
        out_shape=[
            jax.ShapeDtypeStruct((seq, width), bf16),
            jax.ShapeDtypeStruct((8, seq), f32),
        ]
        + [jax.ShapeDtypeStruct((rows, width), bf16)] * (seq // rows),
        scratch_shapes=[pltpu.VMEM((width, seq), bf16)],
        compiler_params=pltpu.CompilerParams(vmem_limit_bytes=56 * 2**20),
        cost_estimate=pl.CostEstimate(
            flops=kernel_cost(16 * seq * seq * width),
            bytes_accessed=8 * seq * width,
            transcendentals=seq * seq * heads,
        ),
        name="attention_forward",
    )(place, qkv, qkv, qkv)


def attention_backward_kernel(
    place_ref,
    q_ref,
    k_ref,
    v_ref,
    mixed_ref,
    lse_ref,
    *refs,
    heads,
    rows,
):
    step = pl.program_id(0)
    dmixed_refs, (out_ref, placed_ref, keys_t_ref, dk_sum, dv_sum, dmixed_ref) = refs[:-6], refs[-6:]
    seq, width = dk_sum.shape
    for slot, slot_ref in enumerate(dmixed_refs):

        @pl.when(step == slot)
        def _(slot_ref=slot_ref):
            dmixed_ref[...] = slot_ref[...]

    @pl.when(step == 0)
    def _():
        keys_t_ref[...] = k_ref[...].T
        dk_sum[...] = jnp.zeros_like(dk_sum)
        dv_sum[...] = jnp.zeros_like(dv_sum)

    queries, dmixed = q_ref[...], dmixed_ref[...]
    queries_t, dmixed_t, mixed_t = queries.T, dmixed.T, mixed_ref[...].T
    product = dmixed_t.astype(f32) * mixed_t.astype(f32)
    lane_head = lax.broadcasted_iota(jnp.int32, (rows, width), 1) // HD
    row_head = lax.broadcasted_iota(jnp.int32, (width, rows), 0) // HD
    none, none_t = jnp.zeros_like(queries), jnp.zeros_like(queries_t)
    lse = lse_ref[...]
    per_head = []
    for head in range(heads):
        per_head.append(
            (
                jnp.where(row_head == head, queries_t, none_t),
                jnp.where(row_head == head, dmixed_t, none_t),
                jnp.where(lane_head == head, queries, none),
                jnp.where(lane_head == head, dmixed, none),
                jnp.sum(product[HD * head : HD * head + HD], axis=0, keepdims=True),
                lse[head : head + 1],
            )
        )

    def chunk(index, dq_t):
        span = pl.ds(pl.multiple_of(index * rows, rows), rows)
        keys, values = k_ref[span, :], v_ref[span, :]
        key_pos = (place_ref[0] ^ index) * rows + lax.broadcasted_iota(jnp.int32, (rows, 1), 0)
        bias = jnp.where(key_pos < place_ref[1], 0.0, -1e30).astype(f32)
        dk, dv = dk_sum[span, :], dv_sum[span, :]
        new_dq_t = []
        for head in range(heads):
            own_q_t, own_do_t, own_q, own_do, delta, own_lse = per_head[head]
            scores = jnp.dot(keys, own_q_t, preferred_element_type=f32)
            probs = jnp.exp2(scores * score_scale_two + bias - own_lse)
            dprobs = jnp.dot(values, own_do_t, preferred_element_type=f32)
            dscores = (probs * (dprobs - delta)).astype(bf16)
            dv = dv + jnp.dot(probs.astype(bf16), own_do, preferred_element_type=f32)
            dk = dk + jnp.dot(dscores, own_q, preferred_element_type=f32)
            own_keys_t = keys_t_ref[HD * head : HD * head + HD, span]
            new_dq_t.append(
                dq_t[head] + jnp.dot(own_keys_t, dscores, preferred_element_type=f32)
            )
        dk_sum[span, :] = dk
        dv_sum[span, :] = dv
        return tuple(new_dq_t)

    start = tuple(jnp.zeros((HD, rows), f32) for _ in range(heads))
    dq_t = jnp.concatenate(lax.fori_loop(0, seq // rows, chunk, start, unroll=4), axis=0)
    own_rows = pl.ds(pl.multiple_of(step * rows, rows), rows)
    out_ref[own_rows, :width] = (dq_t * score_scale).T.astype(bf16)

    @pl.when(step == pl.num_programs(0) - 1)
    def _():
        out_ref[:, width : 2 * width] = (dk_sum[...] * score_scale).astype(bf16)
        out_ref[:, 2 * width :] = dv_sum[...].astype(bf16)
        for slot in range(seq // rows):
            placed_ref[place_ref[0] ^ slot] = out_ref[slot * rows : (slot + 1) * rows, :]


def attention_backward(qkv, mixed, dmixed_slots, lse, place, chunk, chunks):
    seq, width = mixed.shape
    rows = seq // len(dmixed_slots)
    heads = width // HD
    block = pl.BlockSpec((rows, width), lambda i: (i, 0))
    return pl.pallas_call(
        functools.partial(attention_backward_kernel, heads=heads, rows=rows),
        grid=(seq // rows,),
        in_specs=[
            pl.BlockSpec(memory_space=pltpu.SMEM),
            pl.BlockSpec((rows, width), lambda i: (i, chunk)),
            pl.BlockSpec((seq, width), lambda i: (0, chunks + chunk)),
            pl.BlockSpec((seq, width), lambda i: (0, 2 * chunks + chunk)),
            block,
            pl.BlockSpec((8, rows), lambda i: (0, i)),
        ]
        + [pl.BlockSpec((rows, width), lambda i: (0, chunk))] * len(dmixed_slots),
        out_specs=[
            pl.BlockSpec((seq, 3 * width), lambda i: (0, 0)),
            pl.BlockSpec((seq // rows, rows, 3 * width), lambda i: (0, 0, 0)),
        ],
        out_shape=[
            jax.ShapeDtypeStruct((seq, 3 * width), bf16),
            jax.ShapeDtypeStruct((seq // rows, rows, 3 * width), bf16),
        ],
        scratch_shapes=[
            pltpu.VMEM((width, seq), bf16),
            pltpu.VMEM((seq, width), f32),
            pltpu.VMEM((seq, width), f32),
            pltpu.VMEM((rows, width), bf16),
        ],
        compiler_params=pltpu.CompilerParams(vmem_limit_bytes=56 * 2**20),
        cost_estimate=pl.CostEstimate(
            flops=kernel_cost(40 * seq * seq * width),
            bytes_accessed=16 * seq * width,
            transcendentals=seq * seq * heads,
        ),
        name="attention_backward",
    )(place, qkv, qkv, qkv, mixed, lse, *dmixed_slots)


def layer_kernel(
    place_ref,
    tokens_ref,
    cotangent_ref,
    vectors_ref,
    inner_offset_ref,
    *refs,
    chunks,
    groups,
):
    mixed_refs, refs = refs[: chunks * groups], refs[chunks * groups :]
    weight_refs, refs = refs[:2], refs[2:]
    (layer_out_ref, dfirst_ref, sums_ref, inner_sum_ref), refs = refs[:4], refs[4:]
    dmixed_refs, gradient_refs, refs = refs[:groups], refs[groups : groups + 4], refs[groups + 4 :]
    (w_attn, w_inner, w_outer), refs = refs[:3], refs[3:]
    (mixed_ref, hidden_ref, act_ref, douter_ref, dpre_ref, dattn_ref), refs = refs[:6], refs[6:]
    (wide_ref, normed_ref, inverse_ref, total_ref, dmixed_ref, turned_ref, sems) = refs
    rows, width = tokens_ref.shape
    hidden_width = w_inner.shape[1]
    place, length, core, quad = place_ref[0], place_ref[1], place_ref[2], place_ref[3]
    first_row = place * rows

    first_weights, outer_weights = weight_refs
    copies = [
        pltpu.make_async_copy(first_weights.at[:, :width], w_attn, sems.at[0]),
        pltpu.make_async_copy(first_weights.at[:, width:], w_inner, sems.at[1]),
        pltpu.make_async_copy(outer_weights, w_outer, sems.at[2]),
    ]
    for copy in copies:
        copy.start()

    b_attn, g_attn, s_attn = vectors_ref[0:1], vectors_ref[1:2], vectors_ref[2:3]
    b_outer, g_final, s_final = vectors_ref[3:4], vectors_ref[4:5], vectors_ref[5:6]
    chunk_width = mixed_refs[0].shape[1]

    def columns_of(chunk, slot):
        start = ((place ^ slot) * chunks + chunk) * chunk_width
        return pl.ds(pl.multiple_of(start, chunk_width), chunk_width)

    for chunk in range(chunks):
        for slot in range(groups):
            mixed_ref[:, columns_of(chunk, slot)] = mixed_refs[chunk * groups + slot][...]

    copies[0].wait()

    step = 128

    def norm_one(turn, carried):
        span = pl.ds(pl.multiple_of(turn * step, step), step)
        first = (
            tokens_ref[span, :].astype(f32)
            + jnp.dot(mixed_ref[span, :], w_attn[...], preferred_element_type=f32)
            + b_attn
        )
        centered = first - jnp.mean(first, axis=1, keepdims=True)
        inverse = lax.rsqrt(jnp.mean(centered * centered, axis=1, keepdims=True) + norm_eps)
        normed = centered * inverse
        hidden = normed * g_attn + s_attn
        normed_ref[span, :] = normed
        inverse_ref[span, :] = jnp.broadcast_to(inverse, (step, 128))
        total_ref[span, :] = hidden
        hidden_ref[span, :] = hidden.astype(bf16)
        return carried

    lax.fori_loop(0, rows // step, norm_one, 0, unroll=2)

    copies[1].wait()
    block = 512

    def feed_in(turn, carried):
        span = pl.ds(pl.multiple_of(turn * block, block), block)
        pre = (
            jnp.dot(hidden_ref[...], w_inner[:, span], preferred_element_type=f32)
            + inner_offset_ref[:, span]
        )
        normal_cdf = 0.5 * (1.0 + lax.erf(pre * (1.0 / math.sqrt(2.0))))
        act_ref[:, span] = (pre * normal_cdf).astype(bf16)
        slope = normal_cdf + pre * jnp.exp(-0.5 * pre * pre) * (1.0 / math.sqrt(2.0 * math.pi))
        dpre_ref[:, span] = slope.astype(bf16)
        return carried

    lax.fori_loop(0, hidden_width // block, feed_in, 0, unroll=4)

    copies[2].wait()
    narrow = 512

    def feed_out(turn, carried):
        span = pl.ds(pl.multiple_of(turn * narrow, narrow), narrow)
        wide_ref[:, span] = jnp.dot(act_ref[...], w_outer[:, span], preferred_element_type=f32)
        return carried

    lax.fori_loop(0, width // narrow, feed_out, 0, unroll=2)

    def norm_two(turn, carried):
        span = pl.ds(pl.multiple_of(turn * step, step), step)
        second = total_ref[span, :] + wide_ref[span, :] + b_outer
        centered = second - jnp.mean(second, axis=1, keepdims=True)
        inverse = lax.rsqrt(jnp.mean(centered * centered, axis=1, keepdims=True) + norm_eps)
        normed = centered * inverse
        row = first_row + turn * step + lax.broadcasted_iota(jnp.int32, (step, 1), 0)
        valid = jnp.where(row < length, 1.0, 0.0).astype(f32)
        layer_out_ref[span, :] = ((normed * g_final + s_final) * valid).astype(bf16)
        upstream = cotangent_ref[span, :].astype(f32) * valid
        shift_sum, gain_sum, offset_sum = carried
        shift_sum = shift_sum + jnp.sum(upstream, axis=0, keepdims=True)
        gain_sum = gain_sum + jnp.sum(upstream * normed, axis=0, keepdims=True)
        scaled = upstream * g_final
        first_mean = jnp.mean(scaled, axis=1, keepdims=True)
        second_mean = jnp.mean(scaled * normed, axis=1, keepdims=True)
        dsecond = inverse * (scaled - first_mean - normed * second_mean)
        total_ref[span, :] = dsecond
        douter = dsecond.astype(bf16)
        douter_ref[span, :] = douter
        offset_sum = offset_sum + jnp.sum(douter.astype(f32), axis=0, keepdims=True)
        return (shift_sum, gain_sum, offset_sum)

    none = jnp.zeros((1, width), f32)
    shift_sum, gain_sum, offset_sum = lax.fori_loop(
        0, rows // step, norm_two, (none, none, none), unroll=2
    )
    sums_ref[0:1] = offset_sum
    sums_ref[1:2] = gain_sum
    sums_ref[2:3] = shift_sum

    across = (((1,), (1,)), ((), ()))

    def back_out(turn, carried):
        span = pl.ds(pl.multiple_of(turn * block, block), block)
        dact = lax.dot_general(
            douter_ref[...], w_outer[span, :], across, preferred_element_type=f32
        )
        dpre = (dact * dpre_ref[:, span].astype(f32)).astype(bf16)
        dpre_ref[:, span] = dpre
        inner_sum_ref[:, span] = jnp.sum(dpre.astype(f32), axis=0, keepdims=True)
        return carried

    lax.fori_loop(0, hidden_width // block, back_out, 0, unroll=4)

    quads = gradient_refs[0].shape[0]
    slab, outer_slab = width // (2 * quads), hidden_width // (2 * quads)
    down = (((0,), (0,)), ((), ()))

    def leave(first_sem, source, which, to_col, height):
        started = []
        levels = quads.bit_length() - 1
        if which == 0:
            order = [
                sum(((slot >> i) & 1) << (levels - 1 - i) for i in range(levels))
                for slot in range(quads)
            ]
        else:
            order = list(range(quads))
        for side in range(2):
            owner = 1 - core if side == 0 else core
            for slot in range(quads):
                row = pl.multiple_of((2 * (order[slot] ^ quad) + owner) * height, height)
                copy = pltpu.make_async_copy(
                    source.at[pl.ds(row, height), :],
                    gradient_refs[2 * which + side].at[slot, :, to_col : to_col + source.shape[1]],
                    sems.at[first_sem + len(started)],
                )
                copy.start()
                started.append(copy)
        return started

    def outer_gradient(turn, carried):
        span = pl.ds(pl.multiple_of(turn * block, block), block)
        terms = lax.dot_general(
            act_ref[:, span], douter_ref[...], down, preferred_element_type=f32
        )
        w_outer[span, :] = terms.astype(bf16)
        return carried

    lax.fori_loop(0, hidden_width // block, outer_gradient, 0, unroll=4)
    leaving = leave(3, w_outer, 1, 0, outer_slab)

    def back_in(turn, carried):
        span = pl.ds(pl.multiple_of(turn * narrow, narrow), narrow)
        wide_ref[:, span] = lax.dot_general(
            dpre_ref[...], w_inner[span, :], across, preferred_element_type=f32
        )
        return carried

    lax.fori_loop(0, width // narrow, back_in, 0, unroll=2)

    def norm_one_back(turn, carried):
        span = pl.ds(pl.multiple_of(turn * step, step), step)
        dhidden = total_ref[span, :] + wide_ref[span, :]
        normed = normed_ref[span, :]
        inverse = inverse_ref[span, 0:1]
        shift_sum, gain_sum, offset_sum = carried
        shift_sum = shift_sum + jnp.sum(dhidden, axis=0, keepdims=True)
        gain_sum = gain_sum + jnp.sum(dhidden * normed, axis=0, keepdims=True)
        scaled = dhidden * g_attn
        first_mean = jnp.mean(scaled, axis=1, keepdims=True)
        second_mean = jnp.mean(scaled * normed, axis=1, keepdims=True)
        dfirst = inverse * (scaled - first_mean - normed * second_mean)
        dfirst_ref[span, :] = dfirst
        dattn = dfirst.astype(bf16)
        dattn_ref[span, :] = dattn
        offset_sum = offset_sum + jnp.sum(dattn.astype(f32), axis=0, keepdims=True)
        dmixed = lax.dot_general(dattn, w_attn[...], across, preferred_element_type=f32)
        dmixed_ref[span, :] = dmixed.astype(bf16)
        return (shift_sum, gain_sum, offset_sum)

    shift_sum, gain_sum, offset_sum = lax.fori_loop(
        0, rows // step, norm_one_back, (none, none, none), unroll=2
    )
    sums_ref[3:4] = offset_sum
    sums_ref[4:5] = gain_sum
    sums_ref[5:6] = shift_sum
    sums_ref[6:8] = jnp.zeros((2, width), f32)
    group_width = chunks * chunk_width
    for slot in range(groups):
        start = pl.multiple_of((place ^ slot) * group_width, group_width)
        dmixed_refs[slot][...] = dmixed_ref[:, pl.ds(start, group_width)]

    turned_ref[...] = hidden_ref[...].T
    wide_block = 1024

    def inner_gradient(turn, carried):
        span = pl.ds(pl.multiple_of(turn * wide_block, wide_block), wide_block)
        for half in range(width // block):
            rows_of = slice(half * block, (half + 1) * block)
            terms = jnp.dot(turned_ref[rows_of, :], dpre_ref[:, span], preferred_element_type=f32)
            w_inner[rows_of, span] = terms.astype(bf16)
        return carried

    lax.fori_loop(0, hidden_width // wide_block, inner_gradient, 0, unroll=4)
    leaving += leave(3 + len(leaving), w_inner, 0, width, slab)
    turned_ref[...] = mixed_ref[...].T
    for half in range(width // block):
        rows_of = slice(half * block, (half + 1) * block)
        terms = jnp.dot(turned_ref[rows_of, :], dattn_ref[...], preferred_element_type=f32)
        w_attn[rows_of, :] = terms.astype(bf16)
    leaving += leave(3 + len(leaving), w_attn, 0, 0, slab)
    for copy in leaving:
        copy.wait()


def layer_middle(place, tokens, cotangent, vectors, inner_offset, mixed_parts, groups, weights, quads):
    rows, width = tokens.shape
    hidden_width = inner_offset.shape[1]
    chunk_width = mixed_parts[0].shape[1]
    chunks = len(mixed_parts) // groups
    slab, outer_slab = width // (2 * quads), hidden_width // (2 * quads)
    vmem = pl.BlockSpec(memory_space=pltpu.VMEM)
    anywhere = pl.BlockSpec(memory_space=pl.ANY)
    shapes = [
        jax.ShapeDtypeStruct((rows, width), bf16),
        jax.ShapeDtypeStruct((rows, width), f32),
        jax.ShapeDtypeStruct((8, width), f32),
        jax.ShapeDtypeStruct((1, hidden_width), f32),
    ] + [jax.ShapeDtypeStruct((rows, chunks * chunk_width), bf16)] * groups
    gradients = [
        jax.ShapeDtypeStruct((quads, slab, width + hidden_width), bf16),
        jax.ShapeDtypeStruct((quads, outer_slab, width), bf16),
    ]
    gradients = [shape for shape in gradients for _ in range(2)]
    return pl.pallas_call(
        functools.partial(layer_kernel, chunks=chunks, groups=groups),
        in_specs=[pl.BlockSpec(memory_space=pltpu.SMEM)]
        + [vmem] * (4 + chunks * groups)
        + [anywhere] * 2,
        out_specs=[vmem] * len(shapes) + [anywhere] * 4,
        out_shape=shapes + gradients,
        scratch_shapes=[
            pltpu.VMEM((width, width), bf16),
            pltpu.VMEM((width, hidden_width), bf16),
            pltpu.VMEM((hidden_width, width), bf16),
            pltpu.VMEM((rows, width), bf16),
            pltpu.VMEM((rows, width), bf16),
            pltpu.VMEM((rows, hidden_width), bf16),
            pltpu.VMEM((rows, width), bf16),
            pltpu.VMEM((rows, hidden_width), bf16),
            pltpu.VMEM((rows, width), bf16),
            pltpu.VMEM((rows, width), f32),
            pltpu.VMEM((rows, width), f32),
            pltpu.VMEM((rows, 128), f32),
            pltpu.VMEM((rows, width), f32),
            pltpu.VMEM((rows, width), bf16),
            pltpu.VMEM((width, rows), bf16),
            pltpu.SemaphoreType.DMA((3 + 6 * quads,)),
        ],
        compiler_params=pltpu.CompilerParams(vmem_limit_bytes=60 * 2**20),
        cost_estimate=pl.CostEstimate(
            flops=kernel_cost(12 * rows * width * (hidden_width + width)),
            bytes_accessed=4 * width * (2 * hidden_width + width) + 10 * rows * width,
            transcendentals=2 * rows * hidden_width,
        ),
        name="layer_middle",
    )(place, tokens, cotangent, vectors, inner_offset, *mixed_parts, *weights)


def input_kernel(place_ref, dfirst_ref, weights_ref, *refs, slotted, placed, groups):
    slots, parts, (out_ref, rows_ref) = refs[:slotted], refs[slotted:-2], refs[-2:]
    cols = weights_ref.shape[1] // (groups * (slotted // groups + placed))
    chunk = 0
    for first in range(0, slotted, groups):
        for slot in range(groups):
            start = (chunk * groups + (place_ref[0] ^ slot)) * cols
            span = pl.ds(pl.multiple_of(start, cols), cols)
            rows_ref[:, span] = slots[first + slot][...]
        chunk += 1
    for part in parts:
        for group in range(groups):
            start = (chunk * groups + group) * cols
            rows_ref[:, start : start + cols] = part[group]
        chunk += 1
    block = 512

    def columns(turn, carried):
        span = pl.ds(pl.multiple_of(turn * block, block), block)
        terms = lax.dot_general(
            rows_ref[...],
            weights_ref[span, :],
            (((1,), (1,)), ((), ())),
            preferred_element_type=f32,
        )
        out_ref[:, span] = (dfirst_ref[:, span] + terms).astype(bf16)
        return carried

    lax.fori_loop(0, out_ref.shape[1] // block, columns, 0)


def input_gradient(place, dfirst, weights, slots, parts, groups):
    rows, width = dfirst.shape
    vmem = pl.BlockSpec(memory_space=pltpu.VMEM)
    given = list(slots) + list(parts)
    return pl.pallas_call(
        functools.partial(input_kernel, slotted=len(slots), placed=len(parts), groups=groups),
        in_specs=[pl.BlockSpec(memory_space=pltpu.SMEM)] + [vmem] * (2 + len(given)),
        out_specs=vmem,
        out_shape=jax.ShapeDtypeStruct((rows, width), bf16),
        scratch_shapes=[pltpu.VMEM((rows, weights.shape[1]), bf16)],
        compiler_params=pltpu.CompilerParams(vmem_limit_bytes=48 * 2**20),
        cost_estimate=pl.CostEstimate(
            flops=kernel_cost(2 * rows * width * weights.shape[1]),
            bytes_accessed=2 * width * weights.shape[1] + 12 * rows * width,
            transcendentals=0,
        ),
        name="input_gradient",
    )(place, dfirst, weights, *given)


def device_index():
    return lax.axis_index("dp") * lax.axis_size("ctx") + lax.axis_index("ctx")


def bits_of(count):
    return count.bit_length() - 1


def swap(values, bit):
    count = lax.axis_size("dp") * lax.axis_size("ctx")
    return lax.ppermute(values, AXES, [(i, i ^ (1 << bit)) for i in range(count)])


def own_bit(bit):
    return (device_index() >> bit) & 1


def joined(shard, other, bit, axis):
    return jnp.where(
        own_bit(bit) == 1,
        jnp.stack([other, shard], axis=axis),
        jnp.stack([shard, other], axis=axis),
    )


def after(value, *others):
    return lax.optimization_barrier((value,) + others)[0]


def gather_line(block):
    count = lax.axis_size("ctx")
    place = lax.axis_index("ctx")
    held = jnp.broadcast_to(block[None], (count,) + block.shape)
    from_left = from_right = block
    for step in range(1, count):
        from_left, from_right = yield [
            lax.ppermute(from_left, "ctx", [(i, i + 1) for i in range(count - 1)]),
            lax.ppermute(from_right, "ctx", [(i + 1, i) for i in range(count - 1)]),
        ]
        for arrived, source in ((from_left, place - step), (from_right, place + step)):
            inside = (source >= 0) & (source < count)
            held = lax.dynamic_update_index_in_dim(
                held,
                jnp.where(inside, arrived, block),
                jnp.where(inside, source ^ place, 0),
                0,
            )
    return held.reshape((count * block.shape[0],) + block.shape[1:])


def exchange_slots(slots):
    count = lax.axis_size("ctx")
    return [slots[0]] + [
        lax.ppermute(slots[mask], "ctx", [(i, i ^ mask) for i in range(count)])
        for mask in range(1, count)
    ]


def exchange_line(blocks):
    count = lax.axis_size("ctx")
    place = lax.axis_index("ctx")
    arrived = yield [
        lax.ppermute(
            lax.dynamic_index_in_dim(blocks, place ^ mask, 0, keepdims=False),
            "ctx",
            [(i, i ^ mask) for i in range(count)],
        )
        for mask in range(1, count)
    ]
    for mask, value in enumerate(arrived, 1):
        blocks = lax.dynamic_update_index_in_dim(blocks, value, place ^ mask, 0)
    return blocks


def gather_bits(shard, bit_order):
    held = []
    for bit in bit_order:
        (other,) = yield [swap(shard, bit)]
        held = sorted(held + [bit], reverse=True)
        shard = joined(shard, other, bit, held.index(bit))
    return shard.reshape((2 ** len(held),) + shard.shape[len(held) :])


def gather_group(packed, bit_order):
    packed = yield from exchange_line(packed)
    return (yield from gather_bits(packed, bit_order))


def scatter_sum(parts, bit_order, out_dtype, sent):
    left = sorted([bit for bit in bit_order if bit < bits_of(lax.axis_size("ctx"))], reverse=True)
    for bit in bit_order:
        if bit not in left:
            given, parts = [part[1] for part in parts], [part[0] for part in parts]
        else:
            axis, mine = left.index(bit), own_bit(bit)
            given = [lax.dynamic_index_in_dim(part, 1 - mine, axis, False) for part in parts]
            parts = [lax.dynamic_index_in_dim(part, mine, axis, False) for part in parts]
        if bit == bit_order[0]:
            given, kept = total_of(given, parts[0].dtype), total_of(parts, parts[0].dtype)
        else:
            given, kept = given[0] + given[1], parts[0] + parts[1]
        sent.append(given)
        parts = [kept] + (yield [swap(given, bit)])
        if bit in left:
            left.remove(bit)
    return total_of(parts, out_dtype)


def total_of(parts, dtype):
    total = parts[0].astype(f32)
    for part in parts[1:]:
        total = total + part.astype(f32)
    return total.astype(dtype)


def scatter_core(terms, bit):
    mine = own_bit(bit)
    (received,) = yield [swap(lax.dynamic_index_in_dim(terms, 1 - mine, 1, False), bit)]
    kept = lax.dynamic_index_in_dim(terms, mine, 1, False)
    return total_of([kept, received], terms.dtype)


def scatter_at_once(terms, bits):
    masks = range(1, 2 ** len(bits))
    low = min(bits)
    place = (device_index() >> low) & (2 ** len(bits) - 1)
    count = lax.axis_size("dp") * lax.axis_size("ctx")
    received = yield [
        lax.ppermute(
            lax.dynamic_index_in_dim(terms, place ^ mask, 0, keepdims=False),
            AXES,
            [(i, i ^ (mask << low)) for i in range(count)],
        )
        for mask in masks
    ]
    total = lax.dynamic_index_in_dim(terms, place, 0, keepdims=False).astype(f32)
    for value in received:
        total = total + value.astype(f32)
    return total.astype(terms.dtype)


class Process:
    def __init__(self, process):
        self.process = process
        self.arrived = next(process)
        self.result = None

    def advance(self):
        if self.result is not None:
            return
        try:
            self.arrived = self.process.send(self.arrived)
        except StopIteration as stop:
            self.arrived, self.result = [], stop.value

    def finish(self):
        while self.result is None:
            self.advance()
        return self.result


def together(processes, *others):
    flat = [value for process in processes for value in process.arrived]
    flat = list(lax.optimization_barrier(tuple(flat) + tuple(others)))
    for process in processes:
        count = len(process.arrived)
        process.arrived, flat = flat[:count], flat[count:]


def row_sum(values):
    return jnp.sum(values.astype(f32), axis=0)


def local(
    tokens,
    lengths,
    cotangent,
    query_proj,
    query_offset,
    key_proj,
    value_proj,
    value_offset,
    attn_proj,
    attn_offset,
    attn_gain,
    attn_shift,
    inner_proj,
    inner_offset,
    outer_proj,
    outer_offset,
    final_gain,
    final_shift,
):
    n_dp, n_ctx = lax.axis_size("dp"), lax.axis_size("ctx")
    n_dev = n_dp * n_ctx
    dev_bits = bits_of(n_dev)
    ctx_bits = bits_of(n_ctx)
    rows, width = tokens.shape
    seq = rows * n_ctx
    group = width // n_ctx
    part = width // n_dev
    hidden_width = inner_proj.shape[1]
    hidden_part = hidden_width // n_dev
    chunks = group // 128
    place = lax.axis_index("ctx")
    core_bit = ctx_bits
    up_bits = list(range(ctx_bits + 1, dev_bits))
    down_bits = up_bits[::-1]
    ctx_down = list(range(ctx_bits))[::-1]
    ctx_up = list(range(ctx_bits))

    vectors = jnp.concatenate(
        [
            query_offset,
            value_offset,
            attn_offset,
            attn_gain,
            attn_shift,
            outer_offset,
            final_gain,
            final_shift,
            inner_offset,
        ]
    ).astype(bf16)
    triple = jnp.stack([query_proj, key_proj, value_proj], axis=1).astype(bf16)
    by_group = triple.reshape(part, 3, n_ctx, group).transpose(2, 0, 1, 3)
    by_group = by_group.reshape(n_ctx, part, 3 * group)
    vector_rows = -(-vectors.shape[0] // (3 * group))
    vectors = jnp.pad(vectors, (0, vector_rows * 3 * group - vectors.shape[0]))
    vectors = vectors.reshape(vector_rows, 3 * group)
    vectors = jnp.pad(vectors, ((0, 16 - vector_rows), (0, 0)))
    packed = jnp.concatenate(
        [by_group, jnp.broadcast_to(vectors[None], (n_ctx,) + vectors.shape)], axis=1
    )

    first_shard = jnp.concatenate([attn_proj, inner_proj], axis=1).astype(bf16)
    w_first = lax.all_gather(first_shard, AXES, axis=0, tiled=True)
    w_outer = lax.all_gather(outer_proj.astype(bf16), AXES, axis=0, tiled=True)
    line = Process(gather_line(tokens))
    projections = Process(gather_group(packed, down_bits + [core_bit]))
    for turn in range(n_ctx - 1):
        together([line, projections])
        line.advance()
        projections.advance()
    tokens_all, packed = line.result, projections.finish()
    w_group = packed[:, :, :part].reshape(width, 3 * group)
    vectors = packed[:, :, part : part + vector_rows].reshape(n_dev, -1)
    names = [vectors[:, i * part : (i + 1) * part].reshape(width).astype(f32) for i in range(8)]
    b_query, b_value, b_attn, g_attn, s_attn, b_outer, g_final, s_final = names
    b_inner = vectors[:, 8 * part : 8 * part + hidden_part].reshape(1, hidden_width).astype(f32)

    b_group = lax.dynamic_slice_in_dim(
        jnp.stack([b_query, jnp.zeros_like(b_query), b_value]), place * group, group, 1
    ).reshape(3 * group)
    qkv = (jnp.dot(tokens_all, w_group, preferred_element_type=f32) + b_group).astype(bf16)
    where = jnp.stack(
        [place, lengths[0], own_bit(core_bit), lax.axis_index("dp") // 2]
    ).astype(jnp.int32)
    mixed_own, lse, mixed_parts = [], [], []
    for chunk in range(chunks):
        mixed_chunk, lse_chunk, *mixed_slots = attention_forward(qkv, where, rows, chunk, chunks)
        mixed_own.append(mixed_chunk)
        lse.append(lse_chunk)
        mixed_parts += exchange_slots(mixed_slots)

    by_chunk = triple.reshape(part, 3, n_ctx, chunks, 128).transpose(0, 3, 2, 1, 4)
    by_chunk = by_chunk.reshape(part, 3 * width)
    by_chunk, _ = lax.optimization_barrier((by_chunk, qkv))
    w_triple = lax.all_gather(by_chunk, AXES, axis=0, tiled=True)
    none = jnp.zeros_like(b_attn)
    layer_vectors = jnp.stack([b_attn, g_attn, s_attn, b_outer, g_final, s_final, none, none])
    quads = n_dp // 2
    middle = layer_middle(
        where,
        tokens,
        cotangent,
        layer_vectors,
        b_inner,
        mixed_parts,
        n_ctx,
        (w_first, w_outer),
        quads,
    )
    layer_out, dfirst, sums, inner_sum = middle[:4]
    dmixed_slots = exchange_slots(middle[4 : 4 + n_ctx])

    gradients = middle[4 + n_ctx :]
    orders = (
        up_bits + ctx_up,
        down_bits + ctx_down,
    )
    sums_of, given = [], []
    for which, order in enumerate(orders):
        sent, kept = gradients[2 * which : 2 * which + 2]
        shard = sent.shape[0] * sent.shape[1] // 2 ** (dev_bits - 1)
        split = (2,) * (dev_bits - 1) + (shard, sent.shape[2])
        parts = [kept.reshape(split), swap(sent, core_bit).reshape(split)]
        sums_of.append(Process(scatter_sum(parts, order, f32, given)))
    dmixed_slots[0] = after(dmixed_slots[0], w_triple, *given)
    early = [sums[i].reshape(n_dev, part) for i in range(6)] + [inner_sum.reshape(n_dev, -1)]

    dqkv_chunks, dqkv_slots, dqkv_parts, triples, late = [], [], [], [], []
    for chunk in range(chunks):
        dqkv, dqkv_placed = attention_backward(
            qkv, mixed_own[chunk], dmixed_slots, lse[chunk], where, chunk, chunks
        )
        if chunk < chunks - 1:
            slots = [dqkv[slot * rows : (slot + 1) * rows] for slot in range(n_ctx)]
            dqkv_slots += exchange_slots(slots)
            dmixed_slots[0] = after(dmixed_slots[0], *slots)
        else:
            dqkv_parts.append(lax.all_to_all(dqkv_placed, "ctx", 0, 0, tiled=True))
        dqkv_chunks.append(dqkv)

    together(sums_of, dqkv, *dqkv_slots)
    for one in sums_of:
        one.advance()
    for dqkv in dqkv_chunks:
        dqkv = after(dqkv, *given[-2:])
        grad_triple = lax.dot_general(
            tokens_all, dqkv, (((0,), (0,)), ((), ())), preferred_element_type=f32
        ).astype(bf16)
        triples.append(grad_triple.reshape((2,) * (dev_bits - ctx_bits) + (n_ctx, part, 384)))
        late.append(jnp.stack([row_sum(dqkv[:, :128]), row_sum(dqkv[:, 256:])]))
    triple_sum = jnp.concatenate(triples, axis=-1)
    half_sum = triple_sum.reshape((quads, 2) + triple_sum.shape[dev_bits - ctx_bits :])
    half_sum = Process(scatter_core(half_sum, core_bit))
    together(sums_of + [half_sum], *dqkv_parts)
    half_sum.advance()
    triple_sum = Process(scatter_at_once(half_sum.result, up_bits))
    for one in sums_of:
        one.advance()
    dqkv_parts = [after(part, *given[-2:]) for part in dqkv_parts]
    together([one for one in sums_of if one.result is None] + [triple_sum])
    triple_sum.advance()
    triple_sum = Process(exchange_line(triple_sum.result))
    for one in sums_of:
        one.advance()
    triple_sum = triple_sum.finish()
    grad_triple = triple_sum.reshape(n_ctx, part, chunks, 3, 128).transpose(3, 1, 0, 2, 4)
    grad_triple = grad_triple.reshape(3, part, width).astype(f32)
    grad_first, grad_outer = [one.finish() for one in sums_of]
    grad_attn, grad_inner = grad_first[:, :width], grad_first[:, width:]
    late = jnp.concatenate(late, axis=1)
    late = lax.dynamic_update_slice_in_dim(
        jnp.zeros((2, width), f32), late, place * group, 1
    )
    late = late.reshape(2, n_dev, part).transpose(1, 0, 2).reshape(n_dev, 2 * part)
    early = after(jnp.concatenate(early + [late], axis=1), *dqkv_parts)
    early = lax.all_to_all(early, AXES, 0, 0, tiled=True).sum(axis=0)
    late = early[early.shape[0] - 2 * part :].reshape(2, part)
    input_grad = input_gradient(where, dfirst, w_triple, dqkv_slots, dqkv_parts, n_ctx)

    pieces = [early[i * part : (i + 1) * part] for i in range(6)]
    return (
        layer_out,
        input_grad,
        grad_triple[0],
        late[0],
        grad_triple[1],
        grad_triple[2],
        late[1],
        grad_attn,
        pieces[3],
        pieces[4],
        pieces[5],
        grad_inner,
        early[6 * part : 6 * part + hidden_part],
        grad_outer,
        pieces[0],
        pieces[1],
        pieces[2],
    )


def solution(mesh):
    rows, vector = P(AXES, None), P(AXES)
    in_specs = (rows, P("dp"), rows, rows, vector, rows, rows, vector, rows) + (vector,) * 3
    in_specs += (rows, vector, rows) + (vector,) * 3
    out_specs = (rows,) * 3 + (vector, rows, rows, vector, rows) + (vector,) * 3
    out_specs += (rows, vector, rows) + (vector,) * 3
    return jax.shard_map(local, mesh=mesh, in_specs=in_specs, out_specs=out_specs, check_vma=False)
```
